512 devices in a mesh: grp: 16 (over y, x_lo), blk: 32 (over z, x_hi, core).
Axes of the slice: x: 4 (x_hi: 2, x_lo: 2; x = x_hi * 2 + x_lo), y: 8, z: 8, core: 2. Of those that a mesh axis runs over, the one named last changes fastest.
Arguments:
- picture_vectors: bfloat16 [131072, 1152], P(('grp', 'blk')), may hold values from -0.1875 to 0.1875
- caption_vectors: bfloat16 [131072, 1152], P(('grp', 'blk')), may hold values from -0.1875 to 0.1875
- positive_partner: int32 [131072], P(('grp', 'blk')), may hold values from 0 to 131071, as said below
- inverse_warmth: float32 [1], replicated, may hold values from 20 to 60
- affine_offset: float32 [1], replicated, may hold values from -4 to -1
Outputs:
- image_grad: bfloat16 [131072, 1152], P(('grp', 'blk'))
- text_grad: bfloat16 [131072, 1152], P(('grp', 'blk'))
The draws below stay inside these ranges and needn't reach their ends.
Inputs may be any that keep to these rules, and one draw needn't show every extreme that they name: positive_partner[i] names a text of image i's group whose block lies 0 to 7 blocks before image i's block, cyclically over the 32 blocks of the group.
All inputs are finite; a program needn't handle non-finite values.
Results may differ from the reference program's by a relative error of at most 0.0045.
Values may be sent and summed in bfloat16 or wider, within the bound.
A program may use at most 64 MiB of HBM per device.

```python
import math
import jax
import jax.numpy as jnp
from jax import lax

D = 1152
ROWS_DEV = 256
HOPS = 8
GROUP_ROWS = 8192
PAIRS = 131072
N_GRP = 16
N_BLK = 32


def draw_positive_partner(key, part):
    key = jax.random.fold_in(key, 7)
    first, second = jax.random.split(key)
    rows = jnp.arange(PAIRS).astype(jnp.int32)
    group = rows // GROUP_ROWS
    block = rows // ROWS_DEV % N_BLK
    back = jax.random.randint(first, (PAIRS,), 0, HOPS).astype(jnp.int32)
    within = jax.random.randint(second, (PAIRS,), 0, ROWS_DEV).astype(jnp.int32)
    return (group * GROUP_ROWS + (block - back) % N_BLK * ROWS_DEV + within).astype(jnp.int32)


def levels(key, extent, shards, least, top_value):
    factor_of = 1.0
    for position, shards_of in shards:
        draws = jax.random.uniform(jax.random.fold_in(jax.random.fold_in(key, 6), position), (shards_of,), jnp.float32, least / len(shards), top_value / len(shards))
        factor_of = factor_of * jnp.repeat(jnp.exp(draws), extent[position] // shards_of).reshape((-1,) + (1,) * (len(extent) - 1 - position))
    return factor_of


def noise(own_key, dims, spread, bound, cuts=(), held_as=jnp.bfloat16):
    loudness = levels(own_key, dims, cuts, -0.22, 0.18) if cuts else 1.0
    array = jax.random.normal(own_key, dims, jnp.float32) * spread * loudness
    return jnp.minimum(jnp.maximum(array, -bound), bound).astype(held_as)


def setup_inputs(seed: int = 0) -> dict:
    streams_of = jax.random.split(jax.random.key(seed), 6)
    return {
        "picture_vectors": noise(streams_of[0], (PAIRS, D), 0.03, 0.1875, ((0, 512),)),
        "caption_vectors": noise(streams_of[1], (PAIRS, D), 0.03, 0.1875, ((0, 512),)),
        "positive_partner": draw_positive_partner(jax.random.fold_in(streams_of[5], 71), 0),
        "inverse_warmth": jnp.clip(jnp.exp(jax.random.uniform(streams_of[3], (1,), jnp.float32, math.log(20.0), math.log(60.0))), 20.0, 60.0),
        "affine_offset": jnp.clip(jax.random.uniform(streams_of[4], (1,), jnp.float32, -4.0, -1.0), -4.0, -1.0),
    }


def reference(picture_vectors, caption_vectors, positive_partner, inverse_warmth, affine_offset):
    similarity_multiplier = inverse_warmth[0]
    offset = affine_offset[0]
    grouped_image_rows = picture_vectors.reshape(N_GRP, N_BLK, ROWS_DEV, D)
    text_groups = caption_vectors.reshape(N_GRP, N_BLK, ROWS_DEV, D)
    grouped_label_rows = positive_partner.reshape(N_GRP, N_BLK, ROWS_DEV)
    group_ids = jnp.arange(N_GRP).astype(jnp.int32)
    blocks = jnp.arange(N_BLK).astype(jnp.int32)
    column_count = jnp.arange(ROWS_DEV).astype(jnp.int32)

    def one_group(item):
        img_bf, txt_bf, lab, group = item
        img = img_bf.astype(jnp.float32)
        txt = txt_bf.astype(jnp.float32)
        image_acc = jnp.zeros((N_BLK, ROWS_DEV, D), jnp.float32)
        text_acc = jnp.zeros((N_BLK, ROWS_DEV, D), jnp.float32)
        for step in range(HOPS):
            window = jnp.roll(txt, step, axis=0)
            owner = (blocks - step) % N_BLK
            text_ids = (group * GROUP_ROWS + owner[:, None] * ROWS_DEV + column_count[None, :]).astype(jnp.int32)
            sign = jnp.where(lab[:, :, None] == text_ids[:, None, :], 1.0, -1.0).astype(jnp.float32)
            logits = similarity_multiplier * jnp.einsum('kid,kjd->kij', img, window) + offset
            coeff = (-sign * similarity_multiplier * jax.nn.sigmoid(-sign * logits)).astype(jnp.bfloat16).astype(jnp.float32)
            image_acc = image_acc + jnp.einsum('kij,kjd->kid', coeff, window)
            text_part = jnp.einsum('kij,kid->kjd', coeff, img)
            text_acc = text_acc + jnp.roll(text_part, -step, axis=0)
        return image_acc.astype(jnp.bfloat16), text_acc.astype(jnp.bfloat16)

    image_out, text_out = lax.map(one_group, (grouped_image_rows, text_groups, grouped_label_rows, group_ids))
    return image_out.reshape(PAIRS, D), text_out.reshape(PAIRS, D)
```

```python
import functools

import jax
import jax.numpy as jnp
from jax import lax
from jax.experimental import pallas as pl
from jax.experimental.pallas import tpu as pltpu
from jax.sharding import PartitionSpec as P

MESH = pl.DeviceIdType.MESH
HOPS = 8
CHUNKS = 4
TEXT, IMAGE = 0, 1


def kernel(
    n_blk, scale_ref, offset_ref, images, texts, labels, image_out, text_out,
    held, rows_of, column_of, total, stage, local_sem, recv, send, row_recv, row_send,
):
    rows = images.shape[0]
    part = rows // CHUNKS
    n_z = n_blk // 4
    group = lax.axis_index("grp")
    p = lax.axis_index("blk")
    z, x_hi, core = p // 4, (p // 2) % 2, p % 2
    sibling = {"blk": p + 1 - 2 * core}
    partner = {"blk": p + 2 - 4 * x_hi}
    early, late = 1 - x_hi, x_hi
    outer, inner = core, 1 - core

    def along(kind):
        step = 1 - 2 * kind
        return {"blk": lax.rem(z + step + n_z, n_z) * 4 + x_hi * 2 + core}

    loads = [
        pltpu.make_async_copy(texts, held.at[TEXT, 0], local_sem.at[0]),
        pltpu.make_async_copy(images, held.at[IMAGE, 0], local_sem.at[1]),
    ]
    for load in loads:
        load.start()
    barrier = pltpu.get_barrier_semaphore()
    for device in (sibling, partner, along(TEXT), along(IMAGE)):
        pl.semaphore_signal(barrier, inc=1, device_id=device, device_id_type=MESH)

    base = (group * n_blk + p) * rows
    rows_of[TEXT, 0] = base + lax.broadcasted_iota(jnp.int32, (1, rows), 1)
    rows_of[IMAGE, 0] = labels[...]
    column_of[TEXT] = jnp.transpose(jnp.broadcast_to(labels[...], (128, rows)))
    column_of[IMAGE] = base + lax.broadcasted_iota(jnp.int32, (rows, 128), 0)
    for load in loads:
        load.wait()
    pl.semaphore_wait(barrier, 4)

    def copy(route, kind, slot, chunk, to_slot, device):
        span = pl.ds(chunk * part, part)
        return pltpu.make_async_remote_copy(
            src_ref=held.at[kind, slot, span],
            dst_ref=held.at[kind, to_slot, span],
            send_sem=send.at[route, kind, slot, chunk],
            recv_sem=recv.at[kind, to_slot, chunk],
            device_id=device,
            device_id_type=MESH,
        )

    def row_copy(route, kind, slot, to_slot, device):
        return pltpu.make_async_remote_copy(
            src_ref=rows_of.at[kind, slot],
            dst_ref=rows_of.at[kind, to_slot],
            send_sem=row_send.at[route, kind, slot],
            recv_sem=row_recv.at[kind, to_slot],
            device_id=device,
            device_id_type=MESH,
        )

    def by_z(kind, slot, to_slot):
        return (0, kind, slot, to_slot, along(kind))

    def by_x(kind, slot):
        return (1, kind, slot, 2, partner)

    def by_core(kind, slot):
        return (2, kind, slot, slot + jnp.where(kind == outer, 1, -1), sibling)

    def put(transfer, chunk):
        route, kind, slot, to_slot, device = transfer
        copy(route, kind, slot, chunk, to_slot, device).start()
        if chunk == 0:
            row_copy(route, kind, slot, to_slot, device).start()

    def arrived(kind, slot, chunk):
        copy(0, kind, slot, chunk, slot, sibling).wait_recv()
        if chunk == 0:
            row_copy(0, kind, slot, slot, sibling).wait_recv()

    def arrived_whole(kind, slot):
        for chunk in range(CHUNKS):
            arrived(kind, slot, chunk)

    total[...] = jnp.zeros_like(total)
    for chunk in range(CHUNKS):
        put(by_z(early, 0, 4), chunk)
        put(by_z(late, 0, 4), chunk)
        put(by_x(late, 0), chunk)
    for chunk in range(CHUNKS):
        put(by_core(outer, 0), chunk)

    def first_wave(chunk):
        arrived(early, 4, chunk)
        put(by_x(early, 4), chunk)
        put(by_core(early, 4), chunk)
        arrived(late, 4, chunk)
        put(by_core(late, 4), chunk)
        arrived(early, 2, chunk)
        put(by_z(early, 2, 6), chunk)
        put(by_core(early, 2), chunk)
        arrived(outer, 3, chunk)
        put(by_z(outer, 3, 7), chunk)

    def second_wave(chunk):
        arrived(late, 2, chunk)
        put(by_z(late, 2, 6), chunk)
        put(by_core(late, 2), chunk)
        arrived(early, 6, chunk)
        put(by_core(early, 6), chunk)

    def last_wave(chunk):
        arrived(late, 6, chunk)
        put(by_core(late, 6), chunk)

    def odd(kind, outer_slot):
        return jnp.where(kind == outer, outer_slot, outer_slot + 2)

    order = [
        (early, 0), (late, 0), (inner, 1),
        (early, 2), (early, 4), (late, 4), (outer, 3), (inner, 5), (early, odd(early, 1)),
        (late, 2), (late, odd(late, 1)), (early, 6), (early, odd(early, 5)),
        (outer, 7), (late, 6), (late, odd(late, 5)),
    ]

    def before(n):
        if n == 2:
            arrived_whole(inner, 1)
        if n == 3:
            for chunk in range(CHUNKS):
                first_wave(chunk)
        if n == 7:
            second_wave(0)
            arrived_whole(inner, 5)
        if n == 8:
            second_wave(1)
            arrived_whole(*order[8])
        if n == 9:
            second_wave(2)
            last_wave(0)
            second_wave(3)
            last_wave(1)
        if n == 10:
            arrived_whole(*order[10])
        if n == 12:
            last_wave(2)
            arrived_whole(*order[12])
        if n == 13:
            last_wave(3)
            arrived_whole(*order[13])
        if n == 15:
            arrived_whole(*order[15])

    scale = scale_ref[0]
    offset = offset_ref[0]

    def unit(n, carry):
        for step in range(len(order)):
            pl.when(n == step)(functools.partial(before, step))
        kind, slot = order[0]
        for step in range(1, len(order)):
            kind = jnp.where(n == step, order[step][0], kind)
            slot = jnp.where(n == step, order[step][1], slot)
        block = held[kind, slot]
        logits = scale * lax.dot_general(
            held[1 - kind, 0], block, (((1,), (1,)), ((), ())), preferred_element_type=jnp.float32
        ) + offset
        column = jnp.concatenate([column_of[kind]] * (rows // 128), axis=1)
        turn = jnp.where(column == rows_of[kind, slot], -1.0, 1.0)
        coeff = (turn * scale * jax.nn.sigmoid(turn * logits)).astype(jnp.bfloat16)
        total[kind] += jnp.dot(coeff, block, preferred_element_type=jnp.float32)
        return carry

    lax.fori_loop(0, len(order), unit, 0)

    stage[...] = total[...].astype(jnp.bfloat16)
    stores = [
        pltpu.make_async_copy(stage.at[TEXT], image_out, local_sem.at[0]),
        pltpu.make_async_copy(stage.at[IMAGE], text_out, local_sem.at[1]),
    ]
    for store in stores:
        store.start()
    sent = [
        by_z(early, 0, 4), by_z(late, 0, 4), by_x(late, 0), by_core(outer, 0),
        by_x(early, 4), by_core(early, 4), by_core(late, 4),
        by_z(early, 2, 6), by_core(early, 2), by_z(outer, 3, 7),
        by_z(late, 2, 6), by_core(late, 2), by_core(early, 6), by_core(late, 6),
    ]
    for route, kind, slot, to_slot, device in sent:
        for chunk in range(CHUNKS):
            copy(route, kind, slot, chunk, to_slot, device).wait_send()
        row_copy(route, kind, slot, to_slot, device).wait_send()
    for store in stores:
        store.wait()


def solution(mesh):
    n_blk = mesh.shape["blk"]

    def on_device(picture_vectors, caption_vectors, positive_partner, inverse_warmth, affine_offset):
        rows, depth = picture_vectors.shape
        out = jax.ShapeDtypeStruct((rows, depth), jnp.bfloat16)
        whole = pl.BlockSpec(memory_space=pl.ANY)
        scalar = pl.BlockSpec(memory_space=pltpu.SMEM)
        return pl.pallas_call(
            functools.partial(kernel, n_blk),
            out_shape=(out, out),
            in_specs=[scalar, scalar, whole, whole, pl.BlockSpec(memory_space=pltpu.VMEM)],
            out_specs=(whole, whole),
            scratch_shapes=[
                pltpu.VMEM((2, HOPS, rows, depth), jnp.bfloat16),
                pltpu.VMEM((2, HOPS, 1, rows), jnp.int32),
                pltpu.VMEM((2, rows, 128), jnp.int32),
                pltpu.VMEM((2, rows, depth), jnp.float32),
                pltpu.VMEM((2, rows, depth), jnp.bfloat16),
                pltpu.SemaphoreType.DMA((2,)),
                pltpu.SemaphoreType.DMA((2, HOPS, CHUNKS)),
                pltpu.SemaphoreType.DMA((3, 2, HOPS, CHUNKS)),
                pltpu.SemaphoreType.DMA((2, HOPS)),
                pltpu.SemaphoreType.DMA((3, 2, HOPS)),
            ],
            compiler_params=pltpu.CompilerParams(
                collective_id=0, has_side_effects=True, vmem_limit_bytes=48 * 2**20
            ),
            cost_estimate=pl.CostEstimate(
                flops=64 * rows * rows * depth, bytes_accessed=8 * rows * depth, transcendentals=0
            ),
        )(inverse_warmth, affine_offset, picture_vectors, caption_vectors, positive_partner.reshape(1, rows))

    return jax.shard_map(
        on_device,
        mesh=mesh,
        in_specs=(P(("grp", "blk"), None), P(("grp", "blk"), None), P(("grp", "blk")), P(), P()),
        out_specs=(P(("grp", "blk"), None), P(("grp", "blk"), None)),
        check_vma=False,
    )
```

```python
import functools

import jax
import jax.numpy as jnp
from jax import lax
from jax.experimental import pallas as pl
from jax.experimental.pallas import tpu as pltpu
from jax.sharding import PartitionSpec as P

MESH = pl.DeviceIdType.MESH
HOPS = 8
TEXT, IMAGE = 0, 1
VMEM_LIMIT = 40 * 2**20


def kernel(
    n_blk, scale_ref, offset_ref, images, texts, labels, image_out, text_out,
    held, rows_of, column_of, total, local_sem, recv, send, row_recv, row_send,
):
    rows = images.shape[0]
    half_rows, part = rows // 2, rows // 4
    n_z = n_blk // 4
    p = lax.axis_index("blk")
    z, x_hi, core = p // 4, (p // 2) % 2, p % 2
    sibling = {"blk": p + 1 - 2 * core}
    partner = {"blk": p + 2 - 4 * x_hi}
    early, late = 1 - x_hi, x_hi
    outer, inner = core, 1 - core
    up = lax.rem(z + 1, n_z) * 4 + p % 4
    down = lax.rem(z + n_z - 1, n_z) * 4 + p % 4

    def along(kind):
        return {"blk": jnp.where(kind == TEXT, up, down)}

    along_early, along_late, along_outer = along(early), along(late), along(outer)

    barrier = pltpu.get_barrier_semaphore()
    for device in (sibling, partner, along_early, along_late):
        pl.semaphore_signal(barrier, inc=1, device_id=device, device_id_type=MESH)
    loads = [
        pltpu.make_async_copy(texts, held.at[TEXT, 0], local_sem.at[0]),
        pltpu.make_async_copy(images, held.at[IMAGE, 0], local_sem.at[1]),
        pltpu.make_async_copy(labels, rows_of.at[IMAGE, 0], local_sem.at[2]),
    ]
    for load in loads:
        load.start()
    for load in loads:
        load.wait()
    pl.semaphore_wait(barrier, 4)

    def sem_of(kind, slot, q, is_odd):
        if is_odd:
            return recv.at[24 + kind * 8 + slot // 2 * 2 + q // 2]
        return recv.at[kind * 12 + (slot // 2 - 1) * 4 + q]

    def copy(kind, slot, q, n, to_slot, is_odd, device):
        span = pl.ds(q * part, n * part)
        return pltpu.make_async_remote_copy(
            src_ref=held.at[kind, slot, span],
            dst_ref=held.at[kind, to_slot, span],
            send_sem=send.at[0],
            recv_sem=sem_of(kind, to_slot, q - q % 2 if is_odd else q, is_odd),
            device_id=device,
            device_id_type=MESH,
        )

    def row_copy(slot, to_slot, device):
        return pltpu.make_async_remote_copy(
            src_ref=rows_of.at[IMAGE, slot],
            dst_ref=rows_of.at[IMAGE, to_slot],
            send_sem=row_send.at[0],
            recv_sem=row_recv.at[to_slot - 1],
            device_id=device,
            device_id_type=MESH,
        )

    def put(kind, slot, q, n, to_slot, is_odd, device):
        copy(kind, slot, q, n, to_slot, is_odd, device).start()
        if q == 0:
            @pl.when(kind == IMAGE)
            def _():
                row_copy(slot, to_slot, device).start()

    def by_z(kind, slot, q, n, to_slot, device):
        put(kind, slot, q, n, to_slot, to_slot == 7, device)

    def by_x(kind, slot, q, n):
        put(kind, slot, q, n, 2, False, partner)

    def by_core(kind, slot, q, n):
        put(kind, slot, q, n, slot + jnp.where(kind == outer, 1, -1), True, sibling)

    def arrived(kind, slot, q, n, is_odd=False):
        copy(kind, slot, q, n, slot, is_odd, sibling).wait_recv()
        if q == 0:
            @pl.when(kind == IMAGE)
            def _():
                row_copy(slot, slot, sibling).wait_recv()

    for q in range(4):
        by_z(early, 0, q, 1, 4, along_early)
        if q % 2 == 0:
            by_z(late, 0, q, 2, 4, along_late)
            by_x(late, 0, q, 2)
    by_core(outer, 0, 0, 4)

    base = lax.axis_index("grp") * n_blk * rows
    total[...] = jnp.zeros_like(total)
    column_of[IMAGE] = base + p * rows + lax.broadcasted_iota(jnp.int32, (rows, 128), 0)
    for half in range(2):
        column_of[TEXT, pl.ds(half * half_rows, half_rows)] = jnp.transpose(
            jnp.broadcast_to(rows_of[IMAGE, 0, half], (128, half_rows))
        )
        for slot in range(HOPS):
            block = lax.rem(p - slot + n_blk, n_blk)
            rows_of[TEXT, slot, half] = (
                base + block * rows + half * half_rows + lax.broadcasted_iota(jnp.int32, (1, half_rows), 1)
            )

    def first_wave(q):
        arrived(early, 4, q, 1)
        by_x(early, 4, q, 1)
        if q % 2 == 0:
            return
        by_core(early, 4, q - 1, 2)
        arrived(late, 4, q - 1, 2)
        by_core(late, 4, q - 1, 2)
        arrived(early, 2, q - 1, 2)
        by_z(early, 2, q - 1, 2, 6, along_early)
        arrived(outer, 3, q - 1, 2, True)
        by_z(outer, 3, q - 1, 2, 7, along_outer)

    def second_wave(q):
        arrived(late, 2, q, 1)
        by_z(late, 2, q, 1, 6, along_late)
        if q % 2 == 1:
            arrived(early, 6, q - 1, 2)

    def last_wave(q):
        arrived(late, 6, q, 1)
        if q == 1:
            by_core(late, 6, 0, 2)
        if q > 1:
            by_core(late, 6, q, 1)

    def odd(kind, outer_slot):
        return jnp.where(kind == outer, outer_slot, outer_slot + 2)

    def both(kind, slot):
        return (kind, slot, 0, slot, 1)

    order = [
        both(early, 0), both(late, 0), both(inner, 1),
        both(early, 2), both(early, 4), both(late, 4),
        both(outer, 3), both(inner, 5), both(early, odd(early, 1)),
        both(late, 2), both(late, odd(late, 1)), both(early, 6), both(early, odd(early, 5)),
        (late, 6, 0, odd(late, 5), 0), both(outer, 7), (late, 6, 1, odd(late, 5), 1),
    ]

    def before(n):
        if n == 2:
            arrived(inner, 1, 0, 4, True)
        if n == 3:
            for q in range(4):
                first_wave(q)
            by_core(early, 2, 0, 4)
        if n == 6:
            second_wave(0)
        if n == 7:
            arrived(inner, 5, 0, 2, True)
            arrived(inner, 5, 2, 2, True)
        if n == 8:
            second_wave(1)
            arrived(early, odd(early, 1), 0, 4, True)
        if n == 9:
            second_wave(2)
            last_wave(0)
            second_wave(3)
            by_core(late, 2, 0, 4)
            by_core(early, 6, 0, 4)
            last_wave(1)
        if n == 10:
            arrived(late, odd(late, 1), 0, 4, True)
        if n == 11:
            last_wave(2)
        if n == 12:
            arrived(early, odd(early, 5), 0, 4, True)
        if n == 13:
            last_wave(3)
            arrived(late, odd(late, 5), 0, 2, True)
        if n == 14:
            arrived(outer, 7, 0, 2, True)
            arrived(outer, 7, 2, 2, True)
        if n == 15:
            arrived(late, odd(late, 5), 2, 2, True)

    scale = scale_ref[0]
    offset = offset_ref[0]

    def unit(n, carry):
        for step in range(len(order)):
            pl.when(n == step)(functools.partial(before, step))
        picked = list(order[0])
        for step in range(1, len(order)):
            for i in range(len(picked)):
                picked[i] = jnp.where(n == step, order[step][i], picked[i])
        kind, slot_a, half_a, slot_b, half_b = picked

        def piece(slot, half):
            return held[kind, slot, pl.ds(pl.multiple_of(half * half_rows, half_rows), half_rows)]

        block = jnp.concatenate([piece(slot_a, half_a), piece(slot_b, half_b)], axis=0)
        line = jnp.concatenate([rows_of[kind, slot_a, half_a], rows_of[kind, slot_b, half_b]], axis=1)
        logits = scale * lax.dot_general(
            held[1 - kind, 0], block, (((1,), (1,)), ((), ())), preferred_element_type=jnp.float32
        ) + offset
        column = jnp.concatenate([column_of[kind]] * (rows // 128), axis=1)
        turn = jnp.where(column == line, -1.0, 1.0)
        coeff = (turn * scale * jax.nn.sigmoid(turn * logits)).astype(jnp.bfloat16)
        total[kind] += jnp.dot(coeff, block, preferred_element_type=jnp.float32)
        return carry

    lax.fori_loop(0, len(order), unit, 0)

    image_out[...] = total[TEXT].astype(jnp.bfloat16)
    text_out[...] = total[IMAGE].astype(jnp.bfloat16)
    blocks = held.at[:, pl.ds(0, HOPS - 1)]
    pltpu.make_async_remote_copy(
        blocks, blocks, send.at[0], recv.at[0], device_id=sibling, device_id_type=MESH
    ).wait_send()
    for kind, count in ((IMAGE, HOPS), (TEXT, HOPS - 2)):
        @pl.when(outer == kind)
        def _():
            lines = rows_of.at[IMAGE, pl.ds(0, count)]
            pltpu.make_async_remote_copy(
                lines, lines, row_send.at[0], recv.at[0], device_id=sibling, device_id_type=MESH
            ).wait_send()


def solution(mesh):
    n_blk = mesh.shape["blk"]

    def on_device(picture_vectors, caption_vectors, positive_partner, inverse_warmth, affine_offset):
        rows, depth = picture_vectors.shape
        out = jax.ShapeDtypeStruct((rows, depth), jnp.bfloat16)
        whole = pl.BlockSpec(memory_space=pl.ANY)
        scalar = pl.BlockSpec(memory_space=pltpu.SMEM)
        local = pl.BlockSpec(memory_space=pltpu.VMEM)
        operands = [
            pltpu.with_memory_space_constraint(operand, pltpu.HBM)
            for operand in (picture_vectors, caption_vectors, positive_partner.reshape(2, 1, rows // 2))
        ]
        return pl.pallas_call(
            functools.partial(kernel, n_blk),
            out_shape=(out, out),
            in_specs=[scalar, scalar, whole, whole, whole],
            out_specs=(local, local),
            scratch_shapes=[
                pltpu.VMEM((2, HOPS, rows, depth), jnp.bfloat16),
                pltpu.VMEM((2, HOPS, 2, 1, rows // 2), jnp.int32),
                pltpu.VMEM((2, rows, 128), jnp.int32),
                pltpu.VMEM((2, rows, depth), jnp.float32),
                pltpu.SemaphoreType.DMA((3,)),
                pltpu.SemaphoreType.DMA((40,)),
                pltpu.SemaphoreType.DMA((1,)),
                pltpu.SemaphoreType.DMA((HOPS - 1,)),
                pltpu.SemaphoreType.DMA((1,)),
            ],
            compiler_params=pltpu.CompilerParams(
                collective_id=0, has_side_effects=True, vmem_limit_bytes=VMEM_LIMIT
            ),
            cost_estimate=pl.CostEstimate(
                flops=64 * rows * rows * depth, bytes_accessed=8 * rows * depth, transcendentals=0
            ),
        )(inverse_warmth, affine_offset, *operands)

    return jax.shard_map(
        on_device,
        mesh=mesh,
        in_specs=(P(("grp", "blk"), None), P(("grp", "blk"), None), P(("grp", "blk")), P(), P()),
        out_specs=(P(("grp", "blk"), None), P(("grp", "blk"), None)),
        check_vma=False,
    )
```

```python
import functools

import jax
import jax.numpy as jnp
from jax import lax
from jax.experimental import pallas as pl
from jax.experimental.pallas import tpu as pltpu
from jax.sharding import PartitionSpec as P

MESH = pl.DeviceIdType.MESH
HOPS = 8
TEXT, IMAGE = 0, 1
ASIDE = 32
VMEM_LIMIT = 40 * 2**20


def kernel(
    n_blk, scale_ref, offset_ref, images, texts, labels, image_out, text_out,
    held, rows_of, column_of, total, local_sem, recv, send, row_recv, row_send,
):
    rows = images.shape[0]
    half_rows, part = rows // 2, rows // 4
    n_z = n_blk // 4
    p = lax.axis_index("blk")
    z, x_hi, core = p // 4, (p // 2) % 2, p % 2
    sibling = {"blk": p + 1 - 2 * core}
    partner = {"blk": p + 2 - 4 * x_hi}
    early, late = 1 - x_hi, x_hi
    outer, inner = core, 1 - core
    up = lax.rem(z + 1, n_z) * 4 + p % 4
    down = lax.rem(z + n_z - 1, n_z) * 4 + p % 4

    def along(kind):
        return {"blk": jnp.where(kind == TEXT, up, down)}

    along_early, along_late, along_outer = along(early), along(late), along(outer)

    barrier = pltpu.get_barrier_semaphore()
    for device in (sibling, partner, along_early, along_late):
        pl.semaphore_signal(barrier, inc=1, device_id=device, device_id_type=MESH)
    def load(kind, q):
        span = pl.ds(q * part, part)
        return pltpu.make_async_copy(
            (texts, images)[kind].at[span], held.at[kind, 0, span], local_sem.at[kind * 4 + q]
        )

    load_labels = pltpu.make_async_copy(labels, rows_of.at[IMAGE, 0], local_sem.at[8])
    load_labels.start()
    for q in range(4):
        load(TEXT, q).start()
        load(IMAGE, q).start()
    pl.semaphore_wait(barrier, 4)

    def sem_of(kind, slot, q, is_odd):
        if is_odd:
            return recv.at[24 + kind * 8 + slot // 2 * 2 + q // 2]
        return recv.at[kind * 12 + (slot // 2 - 1) * 4 + q]

    def copy_rows(kind, slot, first, count, to_slot, sem, device, send_sem=0):
        span = pl.ds(first, count)
        return pltpu.make_async_remote_copy(
            src_ref=held.at[kind, slot, span],
            dst_ref=held.at[kind, to_slot, span],
            send_sem=send.at[send_sem],
            recv_sem=sem,
            device_id=device,
            device_id_type=MESH,
        )

    def copy(kind, slot, q, n, to_slot, is_odd, device, send_sem=0):
        sem = sem_of(kind, to_slot, q - q % 2 if is_odd else q, is_odd)
        return copy_rows(kind, slot, q * part, n * part, to_slot, sem, device, send_sem)

    def row_copy(slot, to_slot, device):
        return pltpu.make_async_remote_copy(
            src_ref=rows_of.at[IMAGE, slot],
            dst_ref=rows_of.at[IMAGE, to_slot],
            send_sem=row_send.at[0],
            recv_sem=row_recv.at[to_slot - 1],
            device_id=device,
            device_id_type=MESH,
        )

    def put(kind, slot, q, n, to_slot, is_odd, device, send_sem=0):
        copy(kind, slot, q, n, to_slot, is_odd, device, send_sem).start()
        if q == 0:
            @pl.when(kind == IMAGE)
            def _():
                row_copy(slot, to_slot, device).start()

    def by_z(kind, slot, q, n, to_slot, device):
        put(kind, slot, q, n, to_slot, to_slot == 7, device)

    def by_x(kind, slot, q, n):
        put(kind, slot, q, n, 2, False, partner)

    def by_core(kind, slot, q, n, send_sem=0):
        put(kind, slot, q, n, slot + jnp.where(kind == outer, 1, -1), True, sibling, send_sem)

    aside = rows - ASIDE

    def early_aside(kind):
        return copy_rows(kind, 4, aside, ASIDE, 6, sem_of(kind, 6, 3, False), partner)

    def late_aside(kind):
        return copy_rows(kind, 7, 3 * part, part, 5, recv.at[40], partner)

    def late_aside_on():
        return copy_rows(late, 5, 3 * part, part, 6, sem_of(late, 6, 3, False), sibling, 1)

    def arrived(kind, slot, q, n, is_odd=False):
        copy(kind, slot, q, n, slot, is_odd, sibling).wait_recv()
        if q == 0:
            @pl.when(kind == IMAGE)
            def _():
                row_copy(slot, slot, sibling).wait_recv()

    load(TEXT, 0).wait()
    load(IMAGE, 0).wait()
    load_labels.wait()
    row_copy(0, 4, along(IMAGE)).start()
    pl.when(late == IMAGE)(lambda: row_copy(0, 2, partner).start())
    copy(early, 0, 0, 1, 4, False, along_early).start()
    load(TEXT, 1).wait()
    load(IMAGE, 1).wait()
    copy(late, 0, 0, 2, 4, False, along_late).start()
    copy(late, 0, 0, 2, 2, False, partner).start()
    copy(early, 0, 1, 1, 4, False, along_early).start()
    for q in (2, 3):
        load(TEXT, q).wait()
        load(IMAGE, q).wait()
    copy(early, 0, 2, 1, 4, False, along_early).start()
    copy(late, 0, 2, 2, 4, False, along_late).start()
    copy(late, 0, 2, 2, 2, False, partner).start()
    copy(early, 0, 3, 1, 4, False, along_early).start()
    by_core(outer, 0, 0, 4, 1)

    base = lax.axis_index("grp") * n_blk * rows
    total[...] = jnp.zeros_like(total)
    column_of[IMAGE] = base + p * rows + lax.broadcasted_iota(jnp.int32, (rows, 128), 0)
    for half in range(2):
        column_of[TEXT, pl.ds(half * half_rows, half_rows)] = jnp.transpose(
            jnp.broadcast_to(rows_of[IMAGE, 0, half], (128, half_rows))
        )
        for slot in range(HOPS):
            block = lax.rem(p - slot + n_blk, n_blk)
            rows_of[TEXT, slot, half] = (
                base + block * rows + half * half_rows + lax.broadcasted_iota(jnp.int32, (1, half_rows), 1)
            )

    def first_wave(q):
        arrived(early, 4, q, 1)
        by_x(early, 4, q, 1)
        if q % 2 == 0:
            return
        by_core(early, 4, q - 1, 2)
        arrived(late, 4, q - 1, 2)
        by_core(late, 4, q - 1, 2)
        arrived(early, 2, q - 1, 2)
        if q == 1:
            by_z(early, 2, 0, 2, 6, along_early)
        arrived(outer, 3, q - 1, 2, True)
        if q == 1:
            pl.when(outer == late)(lambda: by_z(outer, 3, 0, 2, 7, along_outer))
        if q == 3:
            by_z(outer, 3, 2, 2, 7, along_outer)
            copy_rows(early, 2, 2 * part, aside - 2 * part, 6, sem_of(early, 6, 2, False), along_early).start()
            pl.when(outer == early)(lambda: by_z(outer, 3, 0, 2, 7, along_outer))
            early_aside(late).start()

    def second_wave(q):
        arrived(late, 2, q, 1)
        if q < 3:
            by_z(late, 2, q, 1, 6, along_late)
        else:
            pl.when(late == outer)(lambda: by_z(late, 2, 3, 1, 6, along_late))
        if q == 1:
            arrived(early, 6, 0, 2)
            by_core(early, 6, 0, 2)
        if q % 2 == 1:
            by_core(late, 2, q - 1, 2)

    def early_end():
        copy_rows(early, 6, 2 * part, aside - 2 * part, 6, sem_of(early, 6, 2, False), sibling).wait_recv()
        early_aside(early).wait_recv()
        by_core(early, 6, 2, 2)

    def last_wave(q):
        arrived(late, 6, q, 1)
        if q == 1:
            by_core(late, 6, 0, 2, 1)
        if q == 2:
            by_core(late, 6, 2, 1, 1)
        if q == 3:
            pl.when(late == outer)(lambda: by_core(late, 6, 3, 1, 1))

    def odd(kind, outer_slot):
        return jnp.where(kind == outer, outer_slot, outer_slot + 2)

    def both(kind, slot):
        return (kind, slot, 0, slot, 1)

    order = [
        (both(early, 0), both(late, 0)),
        (both(early, 2), both(early, 4)),
        (both(late, 4), both(outer, 3)),
        (both(inner, 5), both(inner, 1)),
        (both(early, odd(early, 1)), (late, 2, 0, odd(late, 1), 0)),
        ((early, 6, 0, odd(early, 5), 0), (late, 2, 1, odd(late, 1), 1)),
        ((late, 6, 0, odd(late, 5), 0), (early, 6, 1, odd(early, 5), 1)),
        (both(outer, 7), (late, 6, 1, odd(late, 5), 1)),
    ]

    def write(kind):
        for k, out in enumerate((image_out, text_out)):
            @pl.when(kind == k)
            def _():
                out[...] = total[k].astype(jnp.bfloat16)

    def before(n):
        if n == 1:
            for q in range(4):
                first_wave(q)
            by_core(early, 2, 0, 4)
        if n == 3:
            second_wave(0)
            arrived(inner, 5, 0, 2, True)
            arrived(inner, 5, 2, 2, True)
            arrived(inner, 1, 0, 4, True)
        if n == 4:
            second_wave(1)
            arrived(early, odd(early, 1), 0, 4, True)
            arrived(late, odd(late, 1), 0, 2, True)
        if n == 5:
            second_wave(2)
            last_wave(0)

            @pl.when(outer == early)
            def _():
                arrived(early, 7, 2, 2, True)
                late_aside(early).start()

            second_wave(3)
            last_wave(1)
            arrived(early, odd(early, 5), 0, 2, True)
            arrived(late, odd(late, 1), 2, 2, True)
        if n == 6:
            early_end()
            last_wave(2)

            @pl.when(late == outer)
            def _():
                late_aside(late).wait_recv()
                late_aside_on().start()

            arrived(late, odd(late, 5), 0, 2, True)
            arrived(early, odd(early, 5), 2, 2, True)
        if n == 7:
            last_wave(3)
            arrived(outer, 7, 0, 2, True)
            pl.when(outer == late)(lambda: arrived(outer, 7, 2, 2, True))
            pl.when(late == outer)(lambda: arrived(late, 5, 2, 1, True))
            pl.when(late == inner)(lambda: arrived(late, 7, 2, 2, True))

    scale = scale_ref[0]
    offset = offset_ref[0]

    def multiply(n, carry):
        for step in range(len(order)):
            pl.when(n == step)(functools.partial(before, step))

        def piece(kind, slot, half):
            return held[kind, slot, pl.ds(pl.multiple_of(half * half_rows, half_rows), half_rows)]

        units = []
        for u in range(2):
            picked = list(order[0][u])
            for step in range(1, len(order)):
                for i in range(len(picked)):
                    picked[i] = jnp.where(n == step, order[step][u][i], picked[i])
            kind, slot_a, half_a, slot_b, half_b = picked
            block = jnp.concatenate([piece(kind, slot_a, half_a), piece(kind, slot_b, half_b)], axis=0)
            line = jnp.concatenate([rows_of[kind, slot_a, half_a], rows_of[kind, slot_b, half_b]], axis=1)
            logits = scale * lax.dot_general(
                held[1 - kind, 0], block, (((1,), (1,)), ((), ())), preferred_element_type=jnp.float32
            ) + offset
            units.append((kind, block, line, logits))
        grads = []
        for kind, block, line, logits in units:
            column = jnp.concatenate([column_of[kind]] * (rows // 128), axis=1)
            turn = jnp.where(column == line, -1.0, 1.0)
            coeff = (turn * scale * jax.nn.sigmoid(turn * logits)).astype(jnp.bfloat16)
            grads.append((kind, jnp.dot(coeff, block, preferred_element_type=jnp.float32)))
        for kind, grad in grads:
            total[kind] += grad
        return carry

    lax.fori_loop(0, len(order), multiply, 0)

    write(early)
    write(late)
    def all_sent(refs, send_sem):
        pltpu.make_async_remote_copy(
            refs, refs, send_sem, recv.at[0], device_id=sibling, device_id_type=MESH
        ).wait_send()

    all_sent(held.at[:, pl.ds(0, 6)], send.at[0])
    pl.when(late == outer)(lambda: all_sent(held.at[TEXT, pl.ds(0, 3), pl.ds(0, 3 * part)], send.at[1]))
    pl.when(late == inner)(lambda: all_sent(held.at[TEXT, pl.ds(0, 2), pl.ds(0, rows - part // 2)], send.at[1]))
    for kind, count in ((IMAGE, HOPS), (TEXT, HOPS - 2)):
        @pl.when(outer == kind)
        def _():
            all_sent(rows_of.at[IMAGE, pl.ds(0, count)], row_send.at[0])


def solution(mesh):
    n_blk = mesh.shape["blk"]

    def on_device(picture_vectors, caption_vectors, positive_partner, inverse_warmth, affine_offset):
        rows, depth = picture_vectors.shape
        out = jax.ShapeDtypeStruct((rows, depth), jnp.bfloat16)
        whole = pl.BlockSpec(memory_space=pl.ANY)
        scalar = pl.BlockSpec(memory_space=pltpu.SMEM)
        local = pl.BlockSpec(memory_space=pltpu.VMEM)
        operands = [
            pltpu.with_memory_space_constraint(operand, pltpu.HBM)
            for operand in (picture_vectors, caption_vectors, positive_partner.reshape(2, 1, rows // 2))
        ]
        return pl.pallas_call(
            functools.partial(kernel, n_blk),
            out_shape=(out, out),
            in_specs=[scalar, scalar, whole, whole, whole],
            out_specs=(local, local),
            scratch_shapes=[
                pltpu.VMEM((2, HOPS, rows, depth), jnp.bfloat16),
                pltpu.VMEM((2, HOPS, 2, 1, rows // 2), jnp.int32),
                pltpu.VMEM((2, rows, 128), jnp.int32),
                pltpu.VMEM((2, rows, depth), jnp.float32),
                pltpu.SemaphoreType.DMA((9,)),
                pltpu.SemaphoreType.DMA((41,)),
                pltpu.SemaphoreType.DMA((2,)),
                pltpu.SemaphoreType.DMA((HOPS - 1,)),
                pltpu.SemaphoreType.DMA((1,)),
            ],
            compiler_params=pltpu.CompilerParams(
                collective_id=0, has_side_effects=True, vmem_limit_bytes=VMEM_LIMIT
            ),
            cost_estimate=pl.CostEstimate(
                flops=64 * rows * rows * depth, bytes_accessed=8 * rows * depth, transcendentals=0
            ),
        )(inverse_warmth, affine_offset, *operands)

    return jax.shard_map(
        on_device,
        mesh=mesh,
        in_specs=(P(("grp", "blk"), None), P(("grp", "blk"), None), P(("grp", "blk")), P(), P()),
        out_specs=(P(("grp", "blk"), None), P(("grp", "blk"), None)),
        check_vma=False,
    )
```

```python
import functools

import jax
import jax.numpy as jnp
from jax import lax
from jax.experimental import pallas as pl
from jax.experimental.pallas import tpu as pltpu
from jax.sharding import PartitionSpec as P

MESH = pl.DeviceIdType.MESH
HOPS = 8
TEXT, IMAGE = 0, 1
ASIDE = 32
VMEM_LIMIT = 40 * 2**20


def kernel(
    n_blk, scale_ref, offset_ref, images, texts, labels, grads_out,
    held, rows_of, column_of, total, local_sem, recv, send, row_recv, row_send, ready,
):
    rows = images.shape[0]
    half_rows, part = rows // 2, rows // 4
    n_z = n_blk // 4
    p = lax.axis_index("blk")
    z, x_hi, core = p // 4, (p // 2) % 2, p % 2
    sibling = {"blk": p + 1 - 2 * core}
    partner = {"blk": p + 2 - 4 * x_hi}
    early, late = 1 - x_hi, x_hi
    outer, inner = core, 1 - core
    up = lax.rem(z + 1, n_z) * 4 + p % 4
    down = lax.rem(z + n_z - 1, n_z) * 4 + p % 4

    def along(kind):
        return {"blk": jnp.where(kind == TEXT, up, down)}

    along_early, along_late, along_outer = along(early), along(late), along(outer)

    barrier = pltpu.get_barrier_semaphore()
    for device in (sibling, partner, {"blk": down}):
        pl.semaphore_signal(barrier, inc=1, device_id=device, device_id_type=MESH)

    first, last = z == 0, z == n_z - 1

    @pl.when(jnp.logical_not(last))
    def _():
        pl.semaphore_signal(barrier, inc=1, device_id={"blk": up}, device_id_type=MESH)

    def load(kind, q):
        span = pl.ds(q * part, part)
        return pltpu.make_async_copy(
            (texts, images)[kind].at[span], held.at[kind, 0, span], local_sem.at[kind * 4 + q]
        )

    load_labels = pltpu.make_async_copy(labels, rows_of.at[IMAGE, 0], local_sem.at[8])
    load_labels.start()
    for q in range(4):
        load(TEXT, q).start()
        load(IMAGE, q).start()
    pl.semaphore_wait(barrier, jnp.where(first, 3, 4))

    @pl.when(last)
    def _():
        pl.semaphore_signal(ready, inc=1, device_id={"blk": up}, device_id_type=MESH)


    def sem_of(kind, slot, q, is_odd):
        if is_odd:
            return recv.at[24 + kind * 8 + slot // 2 * 2 + q // 2]
        return recv.at[kind * 12 + (slot // 2 - 1) * 4 + q]

    def copy_rows(kind, slot, first, count, to_slot, sem, device, send_sem=0):
        span = pl.ds(first, count)
        return pltpu.make_async_remote_copy(
            src_ref=held.at[kind, slot, span],
            dst_ref=held.at[kind, to_slot, span],
            send_sem=send.at[send_sem],
            recv_sem=sem,
            device_id=device,
            device_id_type=MESH,
        )

    def copy(kind, slot, q, n, to_slot, is_odd, device, send_sem=0):
        sem = sem_of(kind, to_slot, q - q % 2 if is_odd else q, is_odd)
        return copy_rows(kind, slot, q * part, n * part, to_slot, sem, device, send_sem)

    def row_copy(slot, to_slot, device):
        return pltpu.make_async_remote_copy(
            src_ref=rows_of.at[IMAGE, slot],
            dst_ref=rows_of.at[IMAGE, to_slot],
            send_sem=row_send.at[0],
            recv_sem=row_recv.at[to_slot - 1],
            device_id=device,
            device_id_type=MESH,
        )

    def put(kind, slot, q, n, to_slot, is_odd, device, send_sem=0):
        copy(kind, slot, q, n, to_slot, is_odd, device, send_sem).start()
        if q == 0:
            @pl.when(kind == IMAGE)
            def _():
                row_copy(slot, to_slot, device).start()

    def by_z(kind, slot, q, n, to_slot, device):
        put(kind, slot, q, n, to_slot, to_slot == 7, device)

    def by_x(kind, slot, q, n):
        put(kind, slot, q, n, 2, False, partner)

    def by_core(kind, slot, q, n, send_sem=0):
        put(kind, slot, q, n, slot + jnp.where(kind == outer, 1, -1), True, sibling, send_sem)

    aside = rows - ASIDE

    def early_aside(kind):
        return copy_rows(kind, 4, aside, ASIDE, 6, sem_of(kind, 6, 3, False), partner, 2)

    def early_aside_more(kind):
        return copy_rows(kind, 4, 2 * part, aside - 2 * part, 6, sem_of(kind, 6, 2, False), partner, 2)

    def early_rest():
        return copy_rows(early, 2, 2 * part, aside - 2 * part, 6, sem_of(early, 6, 2, False), along_early, 2)

    def late_aside(kind):
        return copy_rows(kind, 7, 3 * part, part, 5, recv.at[40], partner, 2)

    def late_aside_more(kind):
        return copy_rows(kind, 7, 2 * part, part, 5, sem_of(kind, 5, 2, True), partner, 2)

    def late_aside_on(q):
        return copy_rows(late, 5, q * part, part, 6, sem_of(late, 6, q, False), sibling, 1)

    def of_texts(kind, where):
        return jnp.logical_and(kind == TEXT, where)

    def unless(condition):
        return pl.when(jnp.logical_not(condition))

    def arrived(kind, slot, q, n, is_odd=False):
        copy(kind, slot, q, n, slot, is_odd, sibling).wait_recv()
        if q == 0:
            @pl.when(kind == IMAGE)
            def _():
                row_copy(slot, slot, sibling).wait_recv()

    def own_by_z(kind, q, n):
        @pl.when(jnp.logical_or(kind == TEXT, jnp.logical_not(first)))
        def _():
            copy(kind, 0, q, n, 4, False, along(kind)).start()

    def own_by_z_at_first():
        pl.semaphore_wait(ready, 1)
        row_copy(0, 4, {"blk": down}).start()

        @pl.when(early == IMAGE)
        def _():
            for q in range(4):
                copy(IMAGE, 0, q, 1, 4, False, {"blk": down}).start()

        @pl.when(late == IMAGE)
        def _():
            for q in (0, 2):
                copy(IMAGE, 0, q, 2, 4, False, {"blk": down}).start()

    load(TEXT, 0).wait()
    load(IMAGE, 0).wait()
    load_labels.wait()
    pl.when(jnp.logical_not(first))(lambda: row_copy(0, 4, {"blk": down}).start())
    pl.when(late == IMAGE)(lambda: row_copy(0, 2, partner).start())
    own_by_z(early, 0, 1)
    load(TEXT, 1).wait()
    load(IMAGE, 1).wait()
    own_by_z(late, 0, 2)
    copy(late, 0, 0, 2, 2, False, partner).start()
    own_by_z(early, 1, 1)
    for q in (2, 3):
        load(TEXT, q).wait()
        load(IMAGE, q).wait()
    own_by_z(early, 2, 1)
    own_by_z(late, 2, 2)

    def own_by_x_rest():
        copy(late, 0, 2, 2, 2, False, partner).start()

    pl.when(jnp.logical_not(jnp.logical_and(last, late == IMAGE)))(own_by_x_rest)
    own_by_z(early, 3, 1)
    by_core(outer, 0, 0, 4, 1)

    base = lax.axis_index("grp") * n_blk * rows
    total[...] = jnp.zeros_like(total)
    column_of[IMAGE] = base + p * rows + lax.broadcasted_iota(jnp.int32, (rows, 128), 0)
    for half in range(2):
        column_of[TEXT, pl.ds(half * half_rows, half_rows)] = jnp.transpose(
            jnp.broadcast_to(rows_of[IMAGE, 0, half], (128, half_rows))
        )
        for slot in range(HOPS):
            block = lax.rem(p - slot + n_blk, n_blk)
            rows_of[TEXT, slot, half] = (
                base + block * rows + half * half_rows + lax.broadcasted_iota(jnp.int32, (1, half_rows), 1)
            )

    def early_four(q):
        arrived(early, 4, q, 1)
        by_x(early, 4, q, 1)
        if q % 2 == 1:
            by_core(early, 4, q - 1, 2)

    def late_four(q):
        arrived(late, 4, q - 1, 2)
        by_core(late, 4, q - 1, 2)

    def early_two(q):
        arrived(early, 2, q - 1, 2)
        if q == 1:
            by_z(early, 2, 0, 2, 6, along_early)

    def outer_three(q):
        arrived(outer, 3, q - 1, 2, True)
        if q == 1:
            pl.when(outer == late)(lambda: by_z(outer, 3, 0, 2, 7, along_outer))
        if q == 3:
            by_z(outer, 3, 2, 2, 7, along_outer)

    def early_two_rest():
        unless(of_texts(early, last))(lambda: early_rest().start())
        pl.when(outer == early)(lambda: by_z(outer, 3, 0, 2, 7, along_outer))

    def late_four_aside():
        pl.when(of_texts(late, first))(lambda: early_aside_more(late).start())
        early_aside(late).start()

    def first_wave():
        @unless(last)
        def _():
            for q in range(4):
                early_four(q)
                if q % 2 == 1:
                    late_four(q)
                    early_two(q)
                    outer_three(q)
            early_two_rest()
            late_four_aside()

        @pl.when(jnp.logical_and(last, early == TEXT))
        def _():
            for q in range(4):
                early_four(q)
                if q == 3:
                    own_by_x_rest()
                if q % 2 == 1:
                    early_two(q)
                    pl.when(outer == early)(lambda: outer_three(q))
            pl.when(outer == early)(early_two_rest)
            late_four(1)
            late_four(3)
            late_four_aside()

            @pl.when(outer == late)
            def _():
                outer_three(1)
                outer_three(3)
                early_two_rest()

        @pl.when(jnp.logical_and(last, late == TEXT))
        def _():
            early_four(0)
            late_four(1)
            pl.when(outer == late)(lambda: outer_three(1))
            early_four(1)
            late_two(0)
            early_two(1)
            pl.when(outer == early)(lambda: outer_three(1))
            late_four(3)
            late_two(1)
            early_four(2)
            early_four(3)
            late_two(2)
            late_two(3)
            outer_three(3)
            early_two(3)
            early_two_rest()
            late_four_aside()

    def late_two(q):
        arrived(late, 2, q, 1)
        if q < 2:
            by_z(late, 2, q, 1, 6, along_late)
        if q == 2:
            unless(jnp.logical_and(late == inner, of_texts(late, last)))(
                lambda: copy(late, 2, 2, 1, 6, False, along_late, 2).start()
            )
        if q == 3:
            pl.when(late == outer)(lambda: copy(late, 2, 3, 1, 6, False, along_late, 2).start())

    def second_wave(q):
        unless(jnp.logical_and(last, late == TEXT))(lambda: late_two(q))
        if q == 1:
            arrived(early, 6, 0, 2)
            by_core(early, 6, 0, 2)
        if q % 2 == 1:
            by_core(late, 2, q - 1, 2)

    def early_end():
        copy_rows(early, 6, 2 * part, aside - 2 * part, 6, sem_of(early, 6, 2, False), sibling).wait_recv()
        early_aside(early).wait_recv()
        by_core(early, 6, 2, 2)

    def last_wave(q):
        arrived(late, 6, q, 1)
        if q == 1:
            by_core(late, 6, 0, 2, 1)
        if q == 2:
            unless(jnp.logical_and(late == inner, of_texts(late, first)))(lambda: by_core(late, 6, 2, 1, 1))
        if q == 3:
            pl.when(late == outer)(lambda: by_core(late, 6, 3, 1, 1))

    def odd(kind, outer_slot):
        return jnp.where(kind == outer, outer_slot, outer_slot + 2)

    def both(kind, slot):
        return (kind, slot, 0, slot, 1)

    order = [
        (both(early, 0), both(late, 0)),
        (both(early, 2), both(early, 4)),
        (both(late, 4), both(outer, 3)),
        (both(inner, 5), both(inner, 1)),
        (both(early, odd(early, 1)), (late, 2, 0, odd(late, 1), 0)),
        ((early, 6, 0, odd(early, 5), 0), (late, 2, 1, odd(late, 1), 1)),
        ((late, 6, 0, odd(late, 5), 0), (early, 6, 1, odd(early, 5), 1)),
        (both(outer, 7), (late, 6, 1, odd(late, 5), 1)),
    ]

    def before(n):
        if n == 1:
            pl.when(first)(own_by_z_at_first)
            first_wave()
            by_core(early, 2, 0, 4)
        if n == 2:
            second_wave(0)
        if n == 3:
            arrived(inner, 5, 0, 2, True)
            arrived(inner, 5, 2, 2, True)
            arrived(inner, 1, 0, 4, True)
        if n == 4:
            second_wave(1)
            arrived(early, odd(early, 1), 0, 4, True)
            arrived(late, odd(late, 1), 0, 2, True)
        if n == 5:
            second_wave(2)
            last_wave(0)

            @pl.when(outer == early)
            def _():
                arrived(early, 7, 2, 2, True)
                late_aside(early).start()
                pl.when(of_texts(early, first))(lambda: late_aside_more(early).start())

            second_wave(3)
            last_wave(1)
            arrived(early, odd(early, 5), 0, 2, True)
            arrived(late, odd(late, 1), 2, 2, True)
        if n == 6:
            early_end()
            last_wave(2)

            @pl.when(late == outer)
            def _():
                late_aside(late).wait_recv()
                late_aside_on(3).start()

                @pl.when(of_texts(late, first))
                def _():
                    arrived(late, 5, 2, 1, True)
                    late_aside_on(2).start()

            arrived(late, odd(late, 5), 0, 2, True)
            arrived(early, odd(early, 5), 2, 2, True)
        if n == 7:
            last_wave(3)
            arrived(outer, 7, 0, 2, True)
            pl.when(outer == late)(lambda: arrived(outer, 7, 2, 2, True))
            pl.when(jnp.logical_and(late == outer, jnp.logical_not(of_texts(late, first))))(
                lambda: arrived(late, 5, 2, 1, True)
            )
            pl.when(late == inner)(lambda: arrived(late, 7, 2, 2, True))

    scale = scale_ref[0]
    offset = offset_ref[0]

    def multiply(n, carry):
        for step in range(len(order)):
            pl.when(n == step)(functools.partial(before, step))

        def piece(kind, slot, half):
            return held[kind, slot, pl.ds(pl.multiple_of(half * half_rows, half_rows), half_rows)]

        units = []
        for u in range(2):
            picked = list(order[0][u])
            for step in range(1, len(order)):
                for i in range(len(picked)):
                    picked[i] = jnp.where(n == step, order[step][u][i], picked[i])
            kind, slot_a, half_a, slot_b, half_b = picked
            block = jnp.concatenate([piece(kind, slot_a, half_a), piece(kind, slot_b, half_b)], axis=0)
            line = jnp.concatenate([rows_of[kind, slot_a, half_a], rows_of[kind, slot_b, half_b]], axis=1)
            logits = scale * lax.dot_general(
                held[1 - kind, 0], block, (((1,), (1,)), ((), ())), preferred_element_type=jnp.float32
            ) + offset
            units.append((kind, block, line, logits))
        grads = []
        for kind, block, line, logits in units:
            column = jnp.concatenate([column_of[kind]] * (rows // 128), axis=1)
            turn = jnp.where(column == line, -1.0, 1.0)
            coeff = (turn * scale * jax.nn.sigmoid(turn * logits)).astype(jnp.bfloat16)
            grads.append((kind, jnp.dot(coeff, block, preferred_element_type=jnp.float32)))
        for kind, grad in grads:
            total[kind] += grad
        return carry

    lax.fori_loop(0, len(order), multiply, 0)

    grads_out[...] = total[...].astype(jnp.bfloat16)
    def all_sent(refs, send_sem):
        pltpu.make_async_remote_copy(
            refs, refs, send_sem, recv.at[0], device_id=sibling, device_id_type=MESH
        ).wait_send()

    def rows_sent(count, send_sem, also):
        parts = next(n for n in range(1, HOPS) if count % (16 * n) == 0 and count <= rows * n)

        @pl.when(also)
        def _():
            all_sent(held.at[TEXT, pl.ds(0, parts), pl.ds(0, count // parts)], send.at[send_sem])

    all_sent(held.at[:, :, pl.ds(0, 11 * part // 4)], send.at[0])
    late_outer, late_inner = late == outer, late == inner
    more, fewer = of_texts(late, first), of_texts(late, first)
    rows_sent(9 * part, 1, jnp.logical_and(late_outer, jnp.logical_not(more)))
    rows_sent(10 * part, 1, jnp.logical_and(late_outer, more))
    rows_sent(7 * part, 1, jnp.logical_and(late_inner, jnp.logical_not(fewer)))
    rows_sent(6 * part, 1, jnp.logical_and(late_inner, fewer))
    rest = aside - 2 * part
    texts_late = late == TEXT
    changes = [
        (-rest, jnp.logical_and(last, jnp.logical_not(texts_late))),
        (-part, jnp.logical_and(jnp.logical_and(last, texts_late), late_inner)),
        (rest, jnp.logical_and(first, texts_late)),
        (part, jnp.logical_and(jnp.logical_and(first, jnp.logical_not(texts_late)), early == outer)),
    ]
    usual = jnp.bool_(True)
    for change, where in changes:
        rows_sent(4 * part + change, 2, where)
        usual = jnp.logical_and(usual, jnp.logical_not(where))
    rows_sent(4 * part, 2, usual)
    for kind, count in ((IMAGE, HOPS), (TEXT, HOPS - 2)):
        @pl.when(outer == kind)
        def _():
            all_sent(rows_of.at[IMAGE, pl.ds(0, count)], row_send.at[0])


def solution(mesh):
    n_blk = mesh.shape["blk"]

    def on_device(picture_vectors, caption_vectors, positive_partner, inverse_warmth, affine_offset):
        rows, depth = picture_vectors.shape
        whole = pl.BlockSpec(memory_space=pl.ANY)
        scalar = pl.BlockSpec(memory_space=pltpu.SMEM)
        local = pl.BlockSpec(memory_space=pltpu.VMEM)
        operands = [
            pltpu.with_memory_space_constraint(operand, pltpu.HBM)
            for operand in (picture_vectors, caption_vectors, positive_partner.reshape(2, 1, rows // 2))
        ]
        grads = pl.pallas_call(
            functools.partial(kernel, n_blk),
            out_shape=jax.ShapeDtypeStruct((2, rows, depth), jnp.bfloat16),
            in_specs=[scalar, scalar, whole, whole, whole],
            out_specs=local,
            scratch_shapes=[
                pltpu.VMEM((2, HOPS, rows, depth), jnp.bfloat16),
                pltpu.VMEM((2, HOPS, 2, 1, rows // 2), jnp.int32),
                pltpu.VMEM((2, rows, 128), jnp.int32),
                pltpu.VMEM((2, rows, depth), jnp.float32),
                pltpu.SemaphoreType.DMA((9,)),
                pltpu.SemaphoreType.DMA((41,)),
                pltpu.SemaphoreType.DMA((3,)),
                pltpu.SemaphoreType.DMA((HOPS - 1,)),
                pltpu.SemaphoreType.DMA((1,)),
                pltpu.SemaphoreType.REGULAR,
            ],
            compiler_params=pltpu.CompilerParams(
                collective_id=0, has_side_effects=True, vmem_limit_bytes=VMEM_LIMIT
            ),
            cost_estimate=pl.CostEstimate(
                flops=64 * rows * rows * depth, bytes_accessed=8 * rows * depth, transcendentals=0
            ),
        )(inverse_warmth, affine_offset, *operands)
        return grads[TEXT], grads[IMAGE]

    return jax.shard_map(
        on_device,
        mesh=mesh,
        in_specs=(P(("grp", "blk"), None), P(("grp", "blk"), None), P(("grp", "blk")), P(), P()),
        out_specs=(P(("grp", "blk"), None), P(("grp", "blk"), None)),
        check_vma=False,
    )
```

```python
import functools

import jax
import jax.numpy as jnp
from jax import lax
from jax.experimental import pallas as pl
from jax.experimental.pallas import tpu as pltpu
from jax.sharding import PartitionSpec as P

MESH = pl.DeviceIdType.MESH
HOPS = 8
TEXT, IMAGE = 0, 1
ASIDE = 32
VMEM_LIMIT = 40 * 2**20


def kernel(
    n_blk, scale_ref, offset_ref, images, texts, labels, grads_out,
    held, rows_of, column_of, total, local_sem, recv, send, row_recv, row_send, ready,
):
    rows = images.shape[0]
    half_rows, part = rows // 2, rows // 4
    n_z = n_blk // 4
    p = lax.axis_index("blk")
    z, x_hi, core = p // 4, (p // 2) % 2, p % 2
    sibling = {"blk": p + 1 - 2 * core}
    partner = {"blk": p + 2 - 4 * x_hi}
    early, late = 1 - x_hi, x_hi
    outer, inner = core, 1 - core
    up = lax.rem(z + 1, n_z) * 4 + p % 4
    down = lax.rem(z + n_z - 1, n_z) * 4 + p % 4

    def along(kind):
        return {"blk": jnp.where(kind == TEXT, up, down)}

    along_early, along_late, along_outer = along(early), along(late), along(outer)

    def load(kind, q):
        span = pl.ds(q * part, part)
        return pltpu.make_async_copy(
            (texts, images)[kind].at[span], held.at[kind, 0, span], local_sem.at[kind * 4 + q]
        )

    load_labels = pltpu.make_async_copy(labels, rows_of.at[IMAGE, 0], local_sem.at[8])
    load(TEXT, 0).start()
    load(IMAGE, 0).start()
    barrier = pltpu.get_barrier_semaphore()
    for device in (sibling, partner, {"blk": down}):
        pl.semaphore_signal(barrier, inc=1, device_id=device, device_id_type=MESH)

    first, last = z == 0, z == n_z - 1

    @pl.when(jnp.logical_not(last))
    def _():
        pl.semaphore_signal(barrier, inc=1, device_id={"blk": up}, device_id_type=MESH)

    load_labels.start()
    for q in range(1, 4):
        load(TEXT, q).start()
        load(IMAGE, q).start()
    pl.semaphore_wait(barrier, jnp.where(first, 3, 4))

    @pl.when(last)
    def _():
        pl.semaphore_signal(ready, inc=1, device_id={"blk": up}, device_id_type=MESH)


    def sem_of(kind, slot, q, is_odd):
        if is_odd:
            return recv.at[24 + kind * 8 + slot // 2 * 2 + q // 2]
        return recv.at[kind * 12 + (slot // 2 - 1) * 4 + q]

    def copy_rows(kind, slot, first, count, to_slot, sem, device, send_sem=0):
        span = pl.ds(first, count)
        return pltpu.make_async_remote_copy(
            src_ref=held.at[kind, slot, span],
            dst_ref=held.at[kind, to_slot, span],
            send_sem=send.at[send_sem],
            recv_sem=sem,
            device_id=device,
            device_id_type=MESH,
        )

    def copy(kind, slot, q, n, to_slot, is_odd, device, send_sem=0):
        sem = sem_of(kind, to_slot, q - q % 2 if is_odd else q, is_odd)
        return copy_rows(kind, slot, q * part, n * part, to_slot, sem, device, send_sem)

    def row_copy(slot, to_slot, device):
        return pltpu.make_async_remote_copy(
            src_ref=rows_of.at[IMAGE, slot],
            dst_ref=rows_of.at[IMAGE, to_slot],
            send_sem=row_send.at[0],
            recv_sem=row_recv.at[to_slot - 1],
            device_id=device,
            device_id_type=MESH,
        )

    def put(kind, slot, q, n, to_slot, is_odd, device, send_sem=0):
        copy(kind, slot, q, n, to_slot, is_odd, device, send_sem).start()
        if q == 0:
            @pl.when(kind == IMAGE)
            def _():
                row_copy(slot, to_slot, device).start()

    def by_z(kind, slot, q, n, to_slot, device):
        put(kind, slot, q, n, to_slot, to_slot == 7, device)

    def by_x(kind, slot, q, n):
        put(kind, slot, q, n, 2, False, partner)

    def by_core(kind, slot, q, n, send_sem=0):
        put(kind, slot, q, n, slot + jnp.where(kind == outer, 1, -1), True, sibling, send_sem)

    aside = rows - ASIDE

    def early_aside(kind):
        return copy_rows(kind, 4, aside, ASIDE, 6, sem_of(kind, 6, 3, False), partner, 2)

    def early_aside_more(kind):
        return copy_rows(kind, 4, 2 * part, aside - 2 * part, 6, sem_of(kind, 6, 2, False), partner, 2)

    def early_rest():
        return copy_rows(early, 2, 2 * part, aside - 2 * part, 6, sem_of(early, 6, 2, False), along_early, 2)

    def late_aside(kind):
        return copy_rows(kind, 7, 3 * part, part, 5, recv.at[40], partner, 2)

    def late_aside_more(kind):
        return copy_rows(kind, 7, 2 * part, part, 5, sem_of(kind, 5, 2, True), partner, 2)

    def late_aside_on(q):
        return copy_rows(late, 5, q * part, part, 6, sem_of(late, 6, q, False), sibling, 1)

    def of_texts(kind, where):
        return jnp.logical_and(kind == TEXT, where)

    def unless(condition):
        return pl.when(jnp.logical_not(condition))

    def arrived(kind, slot, q, n, is_odd=False):
        copy(kind, slot, q, n, slot, is_odd, sibling).wait_recv()
        if q == 0:
            @pl.when(kind == IMAGE)
            def _():
                row_copy(slot, slot, sibling).wait_recv()

    def own_by_z(kind, q, n):
        @pl.when(jnp.logical_or(kind == TEXT, jnp.logical_not(first)))
        def _():
            copy(kind, 0, q, n, 4, False, along(kind)).start()

    def own_by_z_at_first():
        pl.semaphore_wait(ready, 1)
        row_copy(0, 4, {"blk": down}).start()

        @pl.when(early == IMAGE)
        def _():
            for q in range(4):
                copy(IMAGE, 0, q, 1, 4, False, {"blk": down}).start()

        @pl.when(late == IMAGE)
        def _():
            for q in (0, 2):
                copy(IMAGE, 0, q, 2, 4, False, {"blk": down}).start()

    load(TEXT, 0).wait()
    load(IMAGE, 0).wait()
    own_by_z(early, 0, 1)
    load_labels.wait()
    pl.when(jnp.logical_not(first))(lambda: row_copy(0, 4, {"blk": down}).start())
    pl.when(late == IMAGE)(lambda: row_copy(0, 2, partner).start())
    load(TEXT, 1).wait()
    load(IMAGE, 1).wait()
    own_by_z(late, 0, 2)
    copy(late, 0, 0, 2, 2, False, partner).start()
    own_by_z(early, 1, 1)
    for q in (2, 3):
        load(TEXT, q).wait()
        load(IMAGE, q).wait()
    own_by_z(early, 2, 1)
    own_by_z(late, 2, 2)

    def own_by_x_rest():
        copy(late, 0, 2, 2, 2, False, partner).start()

    pl.when(jnp.logical_not(jnp.logical_and(last, late == IMAGE)))(own_by_x_rest)
    own_by_z(early, 3, 1)
    by_core(outer, 0, 0, 4, 1)

    base = lax.axis_index("grp") * n_blk * rows
    total[...] = jnp.zeros_like(total)
    column_of[IMAGE] = base + p * rows + lax.broadcasted_iota(jnp.int32, (rows, 128), 0)
    for half in range(2):
        column_of[TEXT, pl.ds(half * half_rows, half_rows)] = jnp.transpose(
            jnp.broadcast_to(rows_of[IMAGE, 0, half], (128, half_rows))
        )
        for slot in range(HOPS):
            block = lax.rem(p - slot + n_blk, n_blk)
            rows_of[TEXT, slot, half] = (
                base + block * rows + half * half_rows + lax.broadcasted_iota(jnp.int32, (1, half_rows), 1)
            )

    def early_four(q):
        arrived(early, 4, q, 1)
        by_x(early, 4, q, 1)
        if q % 2 == 1:
            by_core(early, 4, q - 1, 2)

    def late_four(q):
        arrived(late, 4, q - 1, 2)
        by_core(late, 4, q - 1, 2)

    def early_two(q):
        arrived(early, 2, q - 1, 2)
        if q == 1:
            by_z(early, 2, 0, 2, 6, along_early)

    def outer_three(q):
        arrived(outer, 3, q - 1, 2, True)
        if q == 1:
            pl.when(outer == late)(lambda: by_z(outer, 3, 0, 2, 7, along_outer))
        if q == 3:
            by_z(outer, 3, 2, 2, 7, along_outer)

    def early_two_rest():
        unless(of_texts(early, last))(lambda: early_rest().start())
        pl.when(outer == early)(lambda: by_z(outer, 3, 0, 2, 7, along_outer))

    def late_four_aside():
        pl.when(of_texts(late, first))(lambda: early_aside_more(late).start())
        early_aside(late).start()

    def first_wave():
        @unless(last)
        def _():
            for q in range(4):
                early_four(q)
                if q % 2 == 1:
                    late_four(q)
                    early_two(q)
                    outer_three(q)
            early_two_rest()
            late_four_aside()

        @pl.when(jnp.logical_and(last, early == TEXT))
        def _():
            for q in range(4):
                early_four(q)
                if q == 3:
                    own_by_x_rest()
                if q % 2 == 1:
                    early_two(q)
                    pl.when(outer == early)(lambda: outer_three(q))
            pl.when(outer == early)(early_two_rest)
            late_four(1)
            late_four(3)
            late_four_aside()

            @pl.when(outer == late)
            def _():
                outer_three(1)
                outer_three(3)
                early_two_rest()

        @pl.when(jnp.logical_and(last, late == TEXT))
        def _():
            early_four(0)
            late_four(1)
            pl.when(outer == late)(lambda: outer_three(1))
            early_four(1)
            late_two(0)
            early_two(1)
            pl.when(outer == early)(lambda: outer_three(1))
            late_four(3)
            late_two(1)
            early_four(2)
            early_four(3)
            late_two(2)
            late_two(3)
            outer_three(3)
            early_two(3)
            early_two_rest()
            late_four_aside()

    def late_two(q):
        arrived(late, 2, q, 1)
        if q < 2:
            by_z(late, 2, q, 1, 6, along_late)
        if q == 2:
            unless(jnp.logical_and(late == inner, of_texts(late, last)))(
                lambda: copy(late, 2, 2, 1, 6, False, along_late, 2).start()
            )
        if q == 3:
            pl.when(late == outer)(lambda: copy(late, 2, 3, 1, 6, False, along_late, 2).start())

    def second_wave(q):
        unless(jnp.logical_and(last, late == TEXT))(lambda: late_two(q))
        if q == 1:
            arrived(early, 6, 0, 2)
            by_core(early, 6, 0, 2)
        if q % 2 == 1:
            by_core(late, 2, q - 1, 2)

    def early_end():
        copy_rows(early, 6, 2 * part, aside - 2 * part, 6, sem_of(early, 6, 2, False), sibling).wait_recv()
        early_aside(early).wait_recv()
        by_core(early, 6, 2, 2)

    def last_wave(q):
        arrived(late, 6, q, 1)
        if q == 1:
            by_core(late, 6, 0, 2, 1)
        if q == 2:
            unless(jnp.logical_and(late == inner, of_texts(late, first)))(lambda: by_core(late, 6, 2, 1, 1))
        if q == 3:
            pl.when(late == outer)(lambda: by_core(late, 6, 3, 1, 1))

    def odd(kind, outer_slot):
        return jnp.where(kind == outer, outer_slot, outer_slot + 2)

    def both(kind, slot):
        return (kind, slot, 0, slot, 1)

    order = [
        (both(early, 0), both(late, 0)),
        (both(early, 2), both(early, 4)),
        (both(late, 4), both(outer, 3)),
        (both(inner, 5), both(inner, 1)),
        (both(early, odd(early, 1)), (late, 2, 0, odd(late, 1), 0)),
        ((early, 6, 0, odd(early, 5), 0), (late, 2, 1, odd(late, 1), 1)),
        ((late, 6, 0, odd(late, 5), 0), (early, 6, 1, odd(early, 5), 1)),
        (both(outer, 7), (late, 6, 1, odd(late, 5), 1)),
    ]

    def before(n):
        if n == 1:
            pl.when(first)(own_by_z_at_first)
            first_wave()
            by_core(early, 2, 0, 4)
        if n == 2:
            second_wave(0)
        if n == 3:
            arrived(inner, 5, 0, 2, True)
            arrived(inner, 5, 2, 2, True)
            arrived(inner, 1, 0, 4, True)
        if n == 4:
            second_wave(1)
            arrived(early, odd(early, 1), 0, 4, True)
            arrived(late, odd(late, 1), 0, 2, True)
        if n == 5:
            second_wave(2)
            last_wave(0)

            @pl.when(outer == early)
            def _():
                arrived(early, 7, 2, 2, True)
                late_aside(early).start()
                pl.when(of_texts(early, first))(lambda: late_aside_more(early).start())

            second_wave(3)
            last_wave(1)
            arrived(early, odd(early, 5), 0, 2, True)
            arrived(late, odd(late, 1), 2, 2, True)
        if n == 6:
            early_end()
            unless(jnp.logical_and(late == inner, of_texts(late, first)))(lambda: last_wave(2))

            @pl.when(jnp.logical_and(late == outer, jnp.logical_not(of_texts(late, first))))
            def _():
                late_aside(late).wait_recv()
                late_aside_on(3).start()

            arrived(late, odd(late, 5), 0, 2, True)
            arrived(early, odd(early, 5), 2, 2, True)
        if n == 7:
            @pl.when(jnp.logical_and(late == outer, of_texts(late, first)))
            def _():
                late_aside(late).wait_recv()
                late_aside_on(3).start()
                arrived(late, 5, 2, 1, True)
                late_aside_on(2).start()

            pl.when(jnp.logical_and(late == inner, of_texts(late, first)))(lambda: last_wave(2))
            last_wave(3)
            arrived(outer, 7, 0, 2, True)
            pl.when(outer == late)(lambda: arrived(outer, 7, 2, 2, True))
            pl.when(jnp.logical_and(late == outer, jnp.logical_not(of_texts(late, first))))(
                lambda: arrived(late, 5, 2, 1, True)
            )
            pl.when(late == inner)(lambda: arrived(late, 7, 2, 2, True))

    scale = scale_ref[0]
    offset = offset_ref[0]

    def multiply(n, carry):
        for step in range(len(order)):
            pl.when(n == step)(functools.partial(before, step))

        def piece(kind, slot, half):
            return held[kind, slot, pl.ds(pl.multiple_of(half * half_rows, half_rows), half_rows)]

        units = []
        for u in range(2):
            picked = list(order[0][u])
            for step in range(1, len(order)):
                for i in range(len(picked)):
                    picked[i] = jnp.where(n == step, order[step][u][i], picked[i])
            kind, slot_a, half_a, slot_b, half_b = picked
            block = jnp.concatenate([piece(kind, slot_a, half_a), piece(kind, slot_b, half_b)], axis=0)
            line = jnp.concatenate([rows_of[kind, slot_a, half_a], rows_of[kind, slot_b, half_b]], axis=1)
            logits = scale * lax.dot_general(
                held[1 - kind, 0], block, (((1,), (1,)), ((), ())), preferred_element_type=jnp.float32
            ) + offset
            units.append((kind, block, line, logits))
        grads = []
        for kind, block, line, logits in units:
            column = jnp.concatenate([column_of[kind]] * (rows // 128), axis=1)
            turn = jnp.where(column == line, -1.0, 1.0)
            coeff = (turn * scale * jax.nn.sigmoid(turn * logits)).astype(jnp.bfloat16)
            grads.append((kind, jnp.dot(coeff, block, preferred_element_type=jnp.float32)))
        for kind, grad in grads:
            total[kind] += grad
        return carry

    lax.fori_loop(0, len(order), multiply, 0)

    grads_out[...] = total[...].astype(jnp.bfloat16)
    def all_sent(refs, send_sem):
        pltpu.make_async_remote_copy(
            refs, refs, send_sem, recv.at[0], device_id=sibling, device_id_type=MESH
        ).wait_send()

    def rows_sent(count, send_sem, also):
        parts = next(n for n in range(1, HOPS) if count % (16 * n) == 0 and count <= rows * n)

        @pl.when(also)
        def _():
            all_sent(held.at[TEXT, pl.ds(0, parts), pl.ds(0, count // parts)], send.at[send_sem])

    all_sent(held.at[:, :, pl.ds(0, 11 * part // 4)], send.at[0])
    late_outer, late_inner = late == outer, late == inner
    more, fewer = of_texts(late, first), of_texts(late, first)
    rows_sent(9 * part, 1, jnp.logical_and(late_outer, jnp.logical_not(more)))
    rows_sent(10 * part, 1, jnp.logical_and(late_outer, more))
    rows_sent(7 * part, 1, jnp.logical_and(late_inner, jnp.logical_not(fewer)))
    rows_sent(6 * part, 1, jnp.logical_and(late_inner, fewer))
    rest = aside - 2 * part
    texts_late = late == TEXT
    changes = [
        (-rest, jnp.logical_and(last, jnp.logical_not(texts_late))),
        (-part, jnp.logical_and(jnp.logical_and(last, texts_late), late_inner)),
        (rest, jnp.logical_and(first, texts_late)),
        (part, jnp.logical_and(jnp.logical_and(first, jnp.logical_not(texts_late)), early == outer)),
    ]
    usual = jnp.bool_(True)
    for change, where in changes:
        rows_sent(4 * part + change, 2, where)
        usual = jnp.logical_and(usual, jnp.logical_not(where))
    rows_sent(4 * part, 2, usual)
    for kind, count in ((IMAGE, HOPS), (TEXT, HOPS - 2)):
        @pl.when(outer == kind)
        def _():
            all_sent(rows_of.at[IMAGE, pl.ds(0, count)], row_send.at[0])


def solution(mesh):
    n_blk = mesh.shape["blk"]

    def on_device(picture_vectors, caption_vectors, positive_partner, inverse_warmth, affine_offset):
        rows, depth = picture_vectors.shape
        whole = pl.BlockSpec(memory_space=pl.ANY)
        scalar = pl.BlockSpec(memory_space=pltpu.SMEM)
        local = pl.BlockSpec(memory_space=pltpu.VMEM)
        operands = [
            pltpu.with_memory_space_constraint(operand, pltpu.HBM)
            for operand in (picture_vectors, caption_vectors, positive_partner.reshape(2, 1, rows // 2))
        ]
        grads = pl.pallas_call(
            functools.partial(kernel, n_blk),
            out_shape=jax.ShapeDtypeStruct((2, rows, depth), jnp.bfloat16),
            in_specs=[scalar, scalar, whole, whole, whole],
            out_specs=local,
            scratch_shapes=[
                pltpu.VMEM((2, HOPS, rows, depth), jnp.bfloat16),
                pltpu.VMEM((2, HOPS, 2, 1, rows // 2), jnp.int32),
                pltpu.VMEM((2, rows, 128), jnp.int32),
                pltpu.VMEM((2, rows, depth), jnp.float32),
                pltpu.SemaphoreType.DMA((9,)),
                pltpu.SemaphoreType.DMA((41,)),
                pltpu.SemaphoreType.DMA((3,)),
                pltpu.SemaphoreType.DMA((HOPS - 1,)),
                pltpu.SemaphoreType.DMA((1,)),
                pltpu.SemaphoreType.REGULAR,
            ],
            compiler_params=pltpu.CompilerParams(
                collective_id=0, has_side_effects=True, vmem_limit_bytes=VMEM_LIMIT
            ),
            cost_estimate=pl.CostEstimate(
                flops=64 * rows * rows * depth, bytes_accessed=8 * rows * depth, transcendentals=0
            ),
        )(inverse_warmth, affine_offset, *operands)
        return grads[TEXT], grads[IMAGE]

    return jax.shard_map(
        on_device,
        mesh=mesh,
        in_specs=(P(("grp", "blk"), None), P(("grp", "blk"), None), P(("grp", "blk")), P(), P()),
        out_specs=(P(("grp", "blk"), None), P(("grp", "blk"), None)),
        check_vma=False,
    )
```

```python
import functools

import jax
import jax.numpy as jnp
from jax import lax
from jax.experimental import pallas as pl
from jax.experimental.pallas import tpu as pltpu
from jax.sharding import PartitionSpec as P

MESH = pl.DeviceIdType.MESH
HOPS = 8
TEXT, IMAGE = 0, 1
ASIDE = 32
VMEM_LIMIT = 40 * 2**20


def kernel(
    n_blk, scale_ref, offset_ref, images, texts, labels, grads_out,
    held, rows_of, column_of, total, local_sem, recv, send, row_recv, row_send, ready,
):
    rows = images.shape[0]
    half_rows, part = rows // 2, rows // 4
    n_z = n_blk // 4
    p = lax.axis_index("blk")
    z, x_hi, core = p // 4, (p // 2) % 2, p % 2
    sibling = {"blk": p + 1 - 2 * core}
    partner = {"blk": p + 2 - 4 * x_hi}
    early, late = 1 - x_hi, x_hi
    outer, inner = core, 1 - core
    up = lax.rem(z + 1, n_z) * 4 + p % 4
    down = lax.rem(z + n_z - 1, n_z) * 4 + p % 4

    def along(kind):
        return {"blk": jnp.where(kind == TEXT, up, down)}

    along_early, along_late, along_outer = along(early), along(late), along(outer)

    def load(kind, q):
        span = pl.ds(q * part, part)
        return pltpu.make_async_copy(
            (texts, images)[kind].at[span], held.at[kind, 0, span], local_sem.at[kind * 4 + q]
        )

    load_labels = pltpu.make_async_copy(labels, rows_of.at[IMAGE, 0], local_sem.at[8])
    load(TEXT, 0).start()
    load(IMAGE, 0).start()
    barrier = pltpu.get_barrier_semaphore()
    for device in (sibling, partner, {"blk": down}):
        pl.semaphore_signal(barrier, inc=1, device_id=device, device_id_type=MESH)

    first, last = z == 0, z == n_z - 1

    @pl.when(jnp.logical_not(last))
    def _():
        pl.semaphore_signal(barrier, inc=1, device_id={"blk": up}, device_id_type=MESH)

    load_labels.start()
    for q in range(1, 4):
        load(TEXT, q).start()
        load(IMAGE, q).start()
    pl.semaphore_wait(barrier, jnp.where(first, 3, 4))

    @pl.when(last)
    def _():
        pl.semaphore_signal(ready, inc=1, device_id={"blk": up}, device_id_type=MESH)


    def sem_of(kind, slot, q, is_odd):
        if is_odd:
            return recv.at[24 + kind * 8 + slot // 2 * 2 + q // 2]
        return recv.at[kind * 12 + (slot // 2 - 1) * 4 + q]

    def copy_rows(kind, slot, first, count, to_slot, sem, device, send_sem=0):
        span = pl.ds(first, count)
        return pltpu.make_async_remote_copy(
            src_ref=held.at[kind, slot, span],
            dst_ref=held.at[kind, to_slot, span],
            send_sem=send.at[send_sem],
            recv_sem=sem,
            device_id=device,
            device_id_type=MESH,
        )

    def copy(kind, slot, q, n, to_slot, is_odd, device, send_sem=0):
        sem = sem_of(kind, to_slot, q - q % 2 if is_odd else q, is_odd)
        return copy_rows(kind, slot, q * part, n * part, to_slot, sem, device, send_sem)

    def row_copy(slot, to_slot, device):
        return pltpu.make_async_remote_copy(
            src_ref=rows_of.at[IMAGE, slot],
            dst_ref=rows_of.at[IMAGE, to_slot],
            send_sem=row_send.at[0],
            recv_sem=row_recv.at[to_slot - 1],
            device_id=device,
            device_id_type=MESH,
        )

    def put(kind, slot, q, n, to_slot, is_odd, device, send_sem=0):
        copy(kind, slot, q, n, to_slot, is_odd, device, send_sem).start()
        if q == 0:
            @pl.when(kind == IMAGE)
            def _():
                row_copy(slot, to_slot, device).start()

    def by_z(kind, slot, q, n, to_slot, device):
        put(kind, slot, q, n, to_slot, to_slot == 7, device)

    def by_x(kind, slot, q, n):
        put(kind, slot, q, n, 2, False, partner)

    def by_core(kind, slot, q, n, send_sem=0):
        put(kind, slot, q, n, slot + jnp.where(kind == outer, 1, -1), True, sibling, send_sem)

    aside = rows - ASIDE

    def early_aside(kind):
        return copy_rows(kind, 4, aside, ASIDE, 6, sem_of(kind, 6, 3, False), partner, 2)

    def early_aside_more(kind):
        return copy_rows(kind, 4, 2 * part, aside - 2 * part, 6, sem_of(kind, 6, 2, False), partner, 2)

    def early_rest():
        return copy_rows(early, 2, 2 * part, aside - 2 * part, 6, sem_of(early, 6, 2, False), along_early, 2)

    def late_aside(kind):
        return copy_rows(kind, 7, 3 * part, part, 5, recv.at[40], partner, 2)

    def late_aside_more(kind):
        return copy_rows(kind, 7, 2 * part, part, 5, sem_of(kind, 5, 2, True), partner, 2)

    def late_aside_on(q):
        return copy_rows(late, 5, q * part, part, 6, sem_of(late, 6, q, False), sibling, 1)

    def of_texts(kind, where):
        return jnp.logical_and(kind == TEXT, where)

    def unless(condition):
        return pl.when(jnp.logical_not(condition))

    def arrived(kind, slot, q, n, is_odd=False):
        copy(kind, slot, q, n, slot, is_odd, sibling).wait_recv()
        if q == 0:
            @pl.when(kind == IMAGE)
            def _():
                row_copy(slot, slot, sibling).wait_recv()

    def own_by_z(kind, q, n):
        @pl.when(jnp.logical_or(kind == TEXT, jnp.logical_not(first)))
        def _():
            copy(kind, 0, q, n, 4, False, along(kind)).start()

    def own_by_z_at_first():
        pl.semaphore_wait(ready, 1)
        row_copy(0, 4, {"blk": down}).start()

        @pl.when(early == IMAGE)
        def _():
            for q in range(4):
                copy(IMAGE, 0, q, 1, 4, False, {"blk": down}).start()

        @pl.when(late == IMAGE)
        def _():
            for q in (0, 2):
                copy(IMAGE, 0, q, 2, 4, False, {"blk": down}).start()

    load(TEXT, 0).wait()
    load(IMAGE, 0).wait()
    own_by_z(early, 0, 1)
    load_labels.wait()
    pl.when(jnp.logical_not(first))(lambda: row_copy(0, 4, {"blk": down}).start())
    pl.when(late == IMAGE)(lambda: row_copy(0, 2, partner).start())
    load(TEXT, 1).wait()
    load(IMAGE, 1).wait()
    own_by_z(late, 0, 2)
    copy(late, 0, 0, 2, 2, False, partner).start()
    own_by_z(early, 1, 1)
    for q in (2, 3):
        load(TEXT, q).wait()
        load(IMAGE, q).wait()
    own_by_z(early, 2, 1)
    own_by_z(late, 2, 2)

    def own_by_x_rest():
        copy(late, 0, 2, 2, 2, False, partner).start()

    pl.when(jnp.logical_not(jnp.logical_and(last, late == IMAGE)))(own_by_x_rest)
    own_by_z(early, 3, 1)
    by_core(outer, 0, 0, 4, 1)

    base = lax.axis_index("grp") * n_blk * rows
    total[...] = jnp.zeros_like(total)
    column_of[IMAGE] = base + p * rows + lax.broadcasted_iota(jnp.int32, (rows, 128), 0)
    for half in range(2):
        column_of[TEXT, pl.ds(half * half_rows, half_rows)] = jnp.transpose(
            jnp.broadcast_to(rows_of[IMAGE, 0, half], (128, half_rows))
        )
        for slot in range(HOPS):
            block = lax.rem(p - slot + n_blk, n_blk)
            rows_of[TEXT, slot, half] = (
                base + block * rows + half * half_rows + lax.broadcasted_iota(jnp.int32, (1, half_rows), 1)
            )

    def early_four(q):
        arrived(early, 4, q, 1)
        by_x(early, 4, q, 1)
        if q % 2 == 1:
            by_core(early, 4, q - 1, 2)

    def late_four(q):
        arrived(late, 4, q - 1, 2)
        by_core(late, 4, q - 1, 2)

    def early_two(q):
        arrived(early, 2, q - 1, 2)
        if q == 1:
            by_z(early, 2, 0, 2, 6, along_early)

    def outer_three(q):
        arrived(outer, 3, q - 1, 2, True)
        if q == 1:
            pl.when(outer == late)(lambda: by_z(outer, 3, 0, 2, 7, along_outer))
        if q == 3:
            by_z(outer, 3, 2, 2, 7, along_outer)

    def early_two_rest():
        unless(of_texts(early, last))(lambda: early_rest().start())
        pl.when(outer == early)(lambda: by_z(outer, 3, 0, 2, 7, along_outer))

    def late_four_aside():
        pl.when(of_texts(late, first))(lambda: early_aside_more(late).start())
        early_aside(late).start()

    def first_wave():
        @unless(last)
        def _():
            for q in range(4):
                early_four(q)
                if q % 2 == 1:
                    late_four(q)
                    early_two(q)
                    outer_three(q)
            early_two_rest()
            late_four_aside()

        @pl.when(jnp.logical_and(last, early == TEXT))
        def _():
            for q in range(4):
                early_four(q)
                if q == 3:
                    own_by_x_rest()
                if q % 2 == 1:
                    early_two(q)
                    pl.when(outer == early)(lambda: outer_three(q))
            pl.when(outer == early)(early_two_rest)
            late_four(1)
            late_four(3)
            late_four_aside()

            @pl.when(outer == late)
            def _():
                outer_three(1)
                outer_three(3)
                early_two_rest()

        @pl.when(jnp.logical_and(last, late == TEXT))
        def _():
            early_four(0)
            late_four(1)
            pl.when(outer == late)(lambda: outer_three(1))
            early_four(1)
            late_two(0)
            early_two(1)
            pl.when(outer == early)(lambda: outer_three(1))
            late_four(3)
            late_two(1)
            early_four(2)
            early_four(3)
            late_two(2)
            late_two(3)
            outer_three(3)
            early_two(3)
            early_two_rest()
            late_four_aside()

    def late_two(q):
        arrived(late, 2, q, 1)
        if q < 2:
            by_z(late, 2, q, 1, 6, along_late)
        if q == 2:
            unless(jnp.logical_and(late == inner, of_texts(late, last)))(
                lambda: copy(late, 2, 2, 1, 6, False, along_late, 2).start()
            )
        if q == 3:
            pl.when(late == outer)(lambda: copy(late, 2, 3, 1, 6, False, along_late, 2).start())

    def second_wave(q):
        unless(jnp.logical_and(last, late == TEXT))(lambda: late_two(q))
        if q == 1:
            arrived(early, 6, 0, 2)
            by_core(early, 6, 0, 2)
        if q % 2 == 1:
            by_core(late, 2, q - 1, 2)

    def early_end():
        copy_rows(early, 6, 2 * part, aside - 2 * part, 6, sem_of(early, 6, 2, False), sibling).wait_recv()
        early_aside(early).wait_recv()
        by_core(early, 6, 2, 2)

    def last_wave(q):
        arrived(late, 6, q, 1)
        if q == 1:
            by_core(late, 6, 0, 2, 1)
        if q == 2:
            unless(jnp.logical_and(late == inner, of_texts(late, first)))(lambda: by_core(late, 6, 2, 1, 1))
        if q == 3:
            pl.when(late == outer)(lambda: by_core(late, 6, 3, 1, 1))

    def odd(kind, outer_slot):
        return jnp.where(kind == outer, outer_slot, outer_slot + 2)

    def both(kind, slot):
        return (kind, slot, 0, slot, 1)

    order = [
        (both(early, 0), both(late, 0)),
        (both(early, 2), both(early, 4)),
        (both(late, 4), both(outer, 3)),
        (both(inner, 5), both(inner, 1)),
        (both(early, odd(early, 1)), (late, 2, 0, odd(late, 1), 0)),
        ((early, 6, 0, odd(early, 5), 0), (late, 2, 1, odd(late, 1), 1)),
        ((late, 6, 0, odd(late, 5), 0), (early, 6, 1, odd(early, 5), 1)),
        (both(outer, 7), (late, 6, 1, odd(late, 5), 1)),
    ]

    def before(n):
        if n == 1:
            pl.when(first)(own_by_z_at_first)
            first_wave()
            by_core(early, 2, 0, 4)
        if n == 2:
            second_wave(0)
        if n == 3:
            arrived(inner, 5, 0, 2, True)
            arrived(inner, 5, 2, 2, True)
            arrived(inner, 1, 0, 4, True)
        if n == 4:
            second_wave(1)
            arrived(early, odd(early, 1), 0, 4, True)
            arrived(late, odd(late, 1), 0, 2, True)
        if n == 5:
            second_wave(2)
            last_wave(0)

            @pl.when(outer == early)
            def _():
                arrived(early, 7, 2, 2, True)
                late_aside(early).start()
                pl.when(of_texts(early, first))(lambda: late_aside_more(early).start())

            second_wave(3)
            last_wave(1)
            arrived(early, odd(early, 5), 0, 2, True)
            arrived(late, odd(late, 1), 2, 2, True)
        if n == 6:
            early_end()
            unless(jnp.logical_and(late == inner, of_texts(late, first)))(lambda: last_wave(2))

            @pl.when(jnp.logical_and(late == outer, jnp.logical_not(of_texts(late, first))))
            def _():
                late_aside(late).wait_recv()
                late_aside_on(3).start()

            arrived(late, odd(late, 5), 0, 2, True)
            arrived(early, odd(early, 5), 2, 2, True)
        if n == 7:
            @pl.when(jnp.logical_and(late == outer, of_texts(late, first)))
            def _():
                late_aside(late).wait_recv()
                late_aside_on(3).start()
                arrived(late, 5, 2, 1, True)
                late_aside_on(2).start()

            pl.when(jnp.logical_and(late == inner, of_texts(late, first)))(lambda: last_wave(2))
            last_wave(3)
            arrived(outer, 7, 0, 2, True)
            pl.when(outer == late)(lambda: arrived(outer, 7, 2, 2, True))
            pl.when(jnp.logical_and(late == outer, jnp.logical_not(of_texts(late, first))))(
                lambda: arrived(late, 5, 2, 1, True)
            )
            pl.when(late == inner)(lambda: arrived(late, 7, 2, 2, True))

    scale = scale_ref[0]
    offset = offset_ref[0]

    def coefficients(picked):
        kind, slot_a, half_a, slot_b, half_b = picked

        def piece(slot, half):
            return held[kind, slot, pl.ds(pl.multiple_of(half * half_rows, half_rows), half_rows)]

        block = jnp.concatenate([piece(slot_a, half_a), piece(slot_b, half_b)], axis=0)
        line = jnp.concatenate([rows_of[kind, slot_a, half_a], rows_of[kind, slot_b, half_b]], axis=1)
        logits = scale * lax.dot_general(
            held[1 - kind, 0], block, (((1,), (1,)), ((), ())), preferred_element_type=jnp.float32
        ) + offset
        column = jnp.concatenate([column_of[kind]] * (rows // 128), axis=1)
        turn = jnp.where(column == line, -1.0, 1.0)
        return (turn * scale * jax.nn.sigmoid(turn * logits)).astype(jnp.bfloat16), block

    def product(coeff, block):
        return jnp.dot(coeff, block, preferred_element_type=jnp.float32)

    def multiply(n, carry):
        for step in range(len(order) - 1):
            pl.when(n == step)(functools.partial(before, step))
        units = []
        for u in range(2):
            picked = list(order[0][u])
            for step in range(1, len(order) - 1):
                for i in range(len(picked)):
                    picked[i] = jnp.where(n == step, order[step][u][i], picked[i])
            units.append((picked[0], coefficients(picked)))
        grads = [(kind, product(*unit)) for kind, unit in units]
        for kind, grad in grads:
            total[kind] += grad
        return carry

    lax.fori_loop(0, len(order) - 1, multiply, 0)

    @pl.when(outer == late)
    def _():
        grads_out[early] = total[early].astype(jnp.bfloat16)

    before(len(order) - 1)
    unit_a, unit_b = [coefficients(picked) for picked in order[-1]]

    @pl.when(outer == late)
    def _():
        grads_out[late] = (total[late] + product(*unit_a) + product(*unit_b)).astype(jnp.bfloat16)

    @pl.when(outer == early)
    def _():
        grads_out[early] = (total[early] + product(*unit_a)).astype(jnp.bfloat16)
        grads_out[late] = (total[late] + product(*unit_b)).astype(jnp.bfloat16)

    def all_sent(refs, send_sem):
        pltpu.make_async_remote_copy(
            refs, refs, send_sem, recv.at[0], device_id=sibling, device_id_type=MESH
        ).wait_send()

    def rows_sent(count, send_sem, also):
        parts = next(n for n in range(1, HOPS) if count % (16 * n) == 0 and count <= rows * n)

        @pl.when(also)
        def _():
            all_sent(held.at[TEXT, pl.ds(0, parts), pl.ds(0, count // parts)], send.at[send_sem])

    all_sent(held.at[:, :, pl.ds(0, 11 * part // 4)], send.at[0])
    late_outer, late_inner = late == outer, late == inner
    more, fewer = of_texts(late, first), of_texts(late, first)
    rows_sent(9 * part, 1, jnp.logical_and(late_outer, jnp.logical_not(more)))
    rows_sent(10 * part, 1, jnp.logical_and(late_outer, more))
    rows_sent(7 * part, 1, jnp.logical_and(late_inner, jnp.logical_not(fewer)))
    rows_sent(6 * part, 1, jnp.logical_and(late_inner, fewer))
    rest = aside - 2 * part
    texts_late = late == TEXT
    changes = [
        (-rest, jnp.logical_and(last, jnp.logical_not(texts_late))),
        (-part, jnp.logical_and(jnp.logical_and(last, texts_late), late_inner)),
        (rest, jnp.logical_and(first, texts_late)),
        (part, jnp.logical_and(jnp.logical_and(first, jnp.logical_not(texts_late)), early == outer)),
    ]
    usual = jnp.bool_(True)
    for change, where in changes:
        rows_sent(4 * part + change, 2, where)
        usual = jnp.logical_and(usual, jnp.logical_not(where))
    rows_sent(4 * part, 2, usual)
    for kind, count in ((IMAGE, HOPS), (TEXT, HOPS - 2)):
        @pl.when(outer == kind)
        def _():
            all_sent(rows_of.at[IMAGE, pl.ds(0, count)], row_send.at[0])


def solution(mesh):
    n_blk = mesh.shape["blk"]

    def on_device(picture_vectors, caption_vectors, positive_partner, inverse_warmth, affine_offset):
        rows, depth = picture_vectors.shape
        whole = pl.BlockSpec(memory_space=pl.ANY)
        scalar = pl.BlockSpec(memory_space=pltpu.SMEM)
        local = pl.BlockSpec(memory_space=pltpu.VMEM)
        operands = [
            pltpu.with_memory_space_constraint(operand, pltpu.HBM)
            for operand in (picture_vectors, caption_vectors, positive_partner.reshape(2, 1, rows // 2))
        ]
        grads = pl.pallas_call(
            functools.partial(kernel, n_blk),
            out_shape=jax.ShapeDtypeStruct((2, rows, depth), jnp.bfloat16),
            in_specs=[scalar, scalar, whole, whole, whole],
            out_specs=local,
            scratch_shapes=[
                pltpu.VMEM((2, HOPS, rows, depth), jnp.bfloat16),
                pltpu.VMEM((2, HOPS, 2, 1, rows // 2), jnp.int32),
                pltpu.VMEM((2, rows, 128), jnp.int32),
                pltpu.VMEM((2, rows, depth), jnp.float32),
                pltpu.SemaphoreType.DMA((9,)),
                pltpu.SemaphoreType.DMA((41,)),
                pltpu.SemaphoreType.DMA((3,)),
                pltpu.SemaphoreType.DMA((HOPS - 1,)),
                pltpu.SemaphoreType.DMA((1,)),
                pltpu.SemaphoreType.REGULAR,
            ],
            compiler_params=pltpu.CompilerParams(
                collective_id=0, has_side_effects=True, vmem_limit_bytes=VMEM_LIMIT
            ),
            cost_estimate=pl.CostEstimate(
                flops=64 * rows * rows * depth, bytes_accessed=8 * rows * depth, transcendentals=0
            ),
        )(inverse_warmth, affine_offset, *operands)
        return grads[TEXT], grads[IMAGE]

    return jax.shard_map(
        on_device,
        mesh=mesh,
        in_specs=(P(("grp", "blk"), None), P(("grp", "blk"), None), P(("grp", "blk")), P(), P()),
        out_specs=(P(("grp", "blk"), None), P(("grp", "blk"), None)),
        check_vma=False,
    )
```
